256 devices in a mesh: freq: 4 (over x), src: 16 (over y_lo, z), rcv: 4 (over y_hi, core).
Axes of the slice: x: 4, y: 4 (y_hi: 2, y_lo: 2; y = y_hi * 2 + y_lo), z: 8, core: 2. Of those that a mesh axis runs over, the one named last changes fastest.
Arguments:
- direct: float32 [2048, 64, 1024], P(('rcv', 'src'), 'freq'), may hold values from -6 to 6
- reflection: float32 [2, 20, 2048, 2048], P(None, 'freq', 'src', 'rcv'), may hold values from -0.0390625 to 0.0390625
- onset_plus: int32 [2048, 64], P(('rcv', 'src'), 'freq'), may hold values from 256 to 1023
- onset_minus: int32 [2048, 64], P(('src', 'rcv'), 'freq'), may hold values from 256 to 1023
Outputs:
- focus_plus: float32 [2048, 64, 1024], P(('rcv', 'src'), 'freq')
- focus_minus: float32 [2048, 64, 1024], P(('src', 'rcv'), 'freq')
The draws below stay inside these ranges and needn't reach their ends.
All inputs are finite; a program needn't handle non-finite values.
Results may differ from the reference program's by a relative error of at most 0.0001.
Values sent between devices are 32-bit elements; how exact they have to be, the bound alone decides.
A program may use at most 128 MiB of HBM per device.

```python
import math
import jax
import jax.numpy as jnp
from jax import lax

NSRC = 2048
NRCV = 2048
NF = 20
NT = 1024
FIRST_BIN = 32
P_SIZE = 64
ITERS = 2


def place_ends(values, key, least, top_value):
    dims = values.shape
    place = [jax.random.randint(jax.random.fold_in(key, axis), (), 0, dims[axis]) for axis in range(len(dims))]
    values = values.at[tuple(place)].set(least)
    longest = dims.index(max(dims))
    place[longest] = (place[longest] + 1) % dims[longest]
    return values.at[tuple(place)].set(top_value)


def with_spikes(array, own_key, source, target, blocks, factor):
    def block_of(axis_at):
        return (jnp.arange(array.shape[axis_at]) // (array.shape[axis_at] // blocks)).reshape((-1,) + (1,) * (array.ndim - 1 - axis_at))

    near = jax.random.permutation(own_key, blocks)[block_of(target)]
    second = (block_of(target) + blocks // 2) % blocks
    return jnp.where((block_of(source) == near) | (block_of(source) == second), factor * array, array)


def level_of(own_key, dims, shards, low, top_value):
    gain, own = 1.0, jax.random.fold_in(own_key, 6)
    for position, blocks in shards:
        steps = jnp.exp(jax.random.uniform(jax.random.fold_in(own, position), (blocks,), jnp.float32, low / len(shards), top_value / len(shards)))
        gain = gain * jnp.repeat(steps, dims[position] // blocks).reshape([-1 if axis == position else 1 for axis in range(len(dims))])
    return gain


def normal_values(rng, shape, spread, most, cuts=(), kind=jnp.bfloat16):
    array = jax.random.normal(rng, shape, jnp.float32) * spread
    if len(cuts) > 0:
        array = level_of(rng, shape, cuts, -0.22, 0.18) * array
    return jnp.clip(array, min=-most, max=most).astype(kind)


def bell_draw_with(key, dims, width, reach, split, heavy, kind=jnp.bfloat16):
    values = width * jax.random.normal(key, dims, jnp.float32)
    if split:
        values = values * level_of(key, dims, split, -0.22, 0.18)
    return jnp.clip(with_spikes(values, jax.random.fold_in(key, 3), *heavy), -reach, reach).astype(kind)


def setup_inputs(seed: int = 0) -> dict:
    streams_of = jax.random.split(jax.random.key(seed), 5)
    return {
        "direct": normal_values(streams_of[0], (NRCV, P_SIZE, NT), 1.0, 6.0, ((0, 64), (1, 4)), jnp.float32),
        "reflection": bell_draw_with(streams_of[1], (2, NF, NSRC, NRCV), (24 * NRCV) ** -0.5, 0.0390625, ((1, 4), (2, 16), (3, 4)), (2, 3, 16, 2.0), jnp.float32),
        "onset_plus": place_ends(jax.random.randint(streams_of[2], (NRCV, P_SIZE), NT // 4, NT), jax.random.fold_in(streams_of[2], 1), NT // 4, NT - 1).astype(jnp.int32),
        "onset_minus": place_ends(jax.random.randint(streams_of[3], (NSRC, P_SIZE), NT // 4, NT), jax.random.fold_in(streams_of[3], 1), NT // 4, NT - 1).astype(jnp.int32),
    }


HIGHEST = lax.Precision.HIGHEST

def tables(length, lowest, bin_count):
    sample = jnp.arange(length, dtype=jnp.int32)
    orders = lowest + jnp.arange(bin_count, dtype=jnp.int32)
    phases = sample[:, None] * orders[None, :] % length
    angles = phases.astype(jnp.float32) * jnp.float32(2.0 * math.pi / length)
    factor = jnp.float32(math.sqrt(2.0 / length))
    return (factor * jnp.cos(angles), factor * jnp.sin(angles))

def window(onsets, length):
    sample = jnp.arange(length, dtype=jnp.int32)
    return (sample[None, None, :] < onsets[:, :, None]).astype(jnp.float32)

def forward_spectrum(traces, cosine, sine_table):
    real_part = jnp.einsum('spt,tj->jsp', traces, cosine, precision=HIGHEST)
    imag_part = -jnp.einsum('spt,tj->jsp', traces, sine_table, precision=HIGHEST)
    return (real_part, imag_part)

def inverse_spectrum(real_part, imag_part, cosine, sine_table):
    return jnp.einsum('jsp,tj->spt', real_part, cosine, precision=HIGHEST) - jnp.einsum('jsp,tj->spt', imag_part, sine_table, precision=HIGHEST)

def reference(direct, reflection, onset_plus, onset_minus):
    cosine, sine_table = tables(NT, FIRST_BIN, NF)
    keep_plus = window(onset_plus, NT)
    keep_minus = window(onset_minus, NT)
    resp_real = reflection[0]
    resp_imag = reflection[1]
    focus_plus = direct
    focus_minus = jnp.zeros((NSRC, P_SIZE, NT), jnp.float32)
    for repeat in range(ITERS):
        real_part, imag_part = forward_spectrum(focus_plus, cosine, sine_table)
        out_real = jnp.einsum('jsr,jrp->jsp', resp_real, real_part, precision=HIGHEST) - jnp.einsum('jsr,jrp->jsp', resp_imag, imag_part, precision=HIGHEST)
        out_imag = jnp.einsum('jsr,jrp->jsp', resp_real, imag_part, precision=HIGHEST) + jnp.einsum('jsr,jrp->jsp', resp_imag, real_part, precision=HIGHEST)
        focus_minus = keep_minus * inverse_spectrum(out_real, out_imag, cosine, sine_table)
        real_part, imag_part = forward_spectrum(focus_minus, cosine, sine_table)
        back_real = jnp.einsum('jsr,jsp->jrp', resp_real, real_part, precision=HIGHEST) + jnp.einsum('jsr,jsp->jrp', resp_imag, imag_part, precision=HIGHEST)
        back_imag = jnp.einsum('jsr,jsp->jrp', resp_real, imag_part, precision=HIGHEST) - jnp.einsum('jsr,jsp->jrp', resp_imag, real_part, precision=HIGHEST)
        focus_plus = direct + keep_plus * inverse_spectrum(back_real, back_imag, cosine, sine_table)
    return (focus_plus, focus_minus)
```

```python
import math

import jax
import jax.numpy as jnp
import ml_dtypes
import numpy as np
from jax import lax
from jax.experimental import pallas as pl
from jax.experimental.pallas import tpu as pltpu
from jax.sharding import PartitionSpec as P

FIRST_BIN = 32
ITERS = 2
MESH = pl.DeviceIdType.MESH

NF = 20
NX = 4
BL = NF // NX
FP = 16
ST = 32
NT = 1024
NZ = 8
LN = 128
SRC = 128
RCV = 512
ZA = 3
COLS = 2 * NF
WIDE = COLS * FP
STEP = 8
ROWS = STEP * FP


def tables():
    k = (np.arange(NT)[:, None] * (FIRST_BIN + np.arange(NF))[None, :]) % NT
    angle = 2.0 * math.pi * k / NT
    scale = math.sqrt(2.0 / NT)
    table = np.stack([scale * np.cos(angle), -scale * np.sin(angle)], axis=2)
    table = table.reshape(NT, COLS).astype(np.float32)
    high = table.astype(ml_dtypes.bfloat16).astype(np.float32)
    low = (table - high).astype(ml_dtypes.bfloat16).astype(np.float32)
    into = np.zeros((2, NT, LN), np.float32)
    into[0, :, :COLS] = high
    into[0, :, COLS : 2 * COLS] = low
    into[1, :, :COLS] = high
    back = np.zeros((LN, NT), np.float32)
    back[:COLS] = high.T
    back[COLS : 2 * COLS] = high.T
    back[2 * COLS : 3 * COLS] = low.T
    spread = np.zeros((LN, WIDE), np.float32)
    collect = np.zeros((2, WIDE, LN), np.float32)
    for b in range(NF):
        for c in range(2):
            for p in range(FP):
                f, j = b // BL, b % BL
                lane = (f * LN + j * 32 if j < 4 else 4 * LN + f * 32) + c * FP + p
                col = 2 * b + c
                spread[col, lane] = 1
                spread[COLS + col, lane] = 1
                collect[0, lane, col] = 1
                collect[0, lane, 2 * COLS + col] = 1
                collect[1, lane, COLS + col] = 1
    return [a.astype(ml_dtypes.bfloat16) for a in (into, spread, collect, back)]


def halves(x):
    high = x.astype(jnp.bfloat16)
    return high, (x - high.astype(jnp.float32)).astype(jnp.bfloat16)


def mm(a, b):
    return lax.dot_general(a, b, (((1,), (0,)), ((), ())), preferred_element_type=jnp.float32)


def turn(x, lanes):
    lanes = lanes % LN
    return x if lanes == 0 else pltpu.roll(x, lanes, 1)


def pick(parts, i):
    group = lax.broadcasted_iota(jnp.int32, parts[0].shape, 1) // 32
    out = turn(parts[0], -i * 32)
    for k in range(1, 4):
        out = jnp.where(group == k, turn(parts[k], (k - i) * 32), out)
    return out


def own_focus():
    row = lax.broadcasted_iota(jnp.int32, (ROWS, WIDE), 0) % FP
    lane = lax.broadcasted_iota(jnp.int32, (ROWS, WIDE), 1) % FP
    return row == lane


def to_spectrum(x, into, spread):
    high, low = halves(x)
    s = mm(high, into[0]) + mm(low, into[1])
    high, low = halves(s)
    e = mm(high, spread[...]) + mm(low, spread[...])
    e = jnp.where(own_focus(), e, 0.0).reshape(STEP, FP, WIDE)
    return jnp.sum(e, axis=1)


def to_time(z, collect, back):
    high = z.astype(jnp.bfloat16).astype(jnp.float32)
    low = z - high
    own = own_focus()

    def rows(v):
        v = jnp.broadcast_to(v[:, None, :], (STEP, FP, WIDE)).reshape(ROWS, WIDE)
        return jnp.where(own, v, 0.0).astype(jnp.bfloat16)

    g = mm(rows(high), collect[0]) + mm(rows(low), collect[1])
    return mm(g.astype(jnp.bfloat16), back[...])


def is_real(shape):
    return lax.broadcasted_iota(jnp.int32, shape, 1) % 32 < FP


def swap_parts(x, real):
    return jnp.where(real, turn(x, -FP), turn(x, FP))


def kernel(
    direct, refl, on_plus, on_minus, into, spread, collect, back,
    out_plus, out_minus,
    r_high, r_low, t_high, t_low, onset, spec, piece, landed,
    xs, y, r4a, r4b, cs, h, rsy, rsz, rsp, rsf, send_sem, recv_sem,
):
    f = lax.axis_index("freq")
    src = lax.axis_index("src")
    rcv = lax.axis_index("rcv")
    line = src // NZ
    z = src % NZ
    high_y = rcv // 2
    core = rcv % 2
    right = (f, line * NZ + (z + 1) % NZ, rcv)
    left = (f, line * NZ + (z + NZ - 1) % NZ, rcv)
    across = (f, (1 - line) * NZ + z, rcv)
    sibling = (f, src, high_y * 2 + 1 - core)
    opposite = (f, src, (1 - high_y) * 2 + core)
    freqs = [None] + [(f + o) % NX for o in range(1, NX)]
    peers = [right, left, across, sibling, opposite] + [(q, src, rcv) for q in freqs[1:]]

    barrier = pltpu.get_barrier_semaphore()
    for peer in peers:
        pl.semaphore_signal(barrier, inc=1, device_id=peer, device_id_type=MESH)

    names = {}

    def copy(name, source, target, device):
        n = names.setdefault(name, len(names))
        return pltpu.make_async_remote_copy(
            src_ref=source, dst_ref=target, send_sem=send_sem.at[n], recv_sem=recv_sem.at[n],
            device_id=device, device_id_type=MESH,
        )

    def rows_at(on_line, dist):
        block = on_line * NZ + (z + dist + NZ) % NZ
        return pl.ds(pl.multiple_of(block * ST, ST), ST)

    def half_at(on_line, dist, part):
        block = on_line * NZ + (z + dist + NZ) % NZ
        return pl.ds(pl.multiple_of(block * ST + part * (ST // 2), ST // 2), ST // 2)

    def rcv_rows(hy, c):
        return pl.ds(pl.multiple_of((hy * 2 + c) * ST, ST), ST)

    def prepare(j, _):
        block = refl[:, j].reshape(2 * SRC, RCV)
        high, low = halves(block)
        r_high[j] = high
        r_low[j] = low
        high, low = halves(block.T)
        t_high[j] = high
        t_low[j] = low
        return 0

    lax.fori_loop(0, BL, prepare, 0)
    eye = (
        lax.broadcasted_iota(jnp.int32, (ST, FP, FP), 1)
        == lax.broadcasted_iota(jnp.int32, (ST, FP, FP), 2)
    )
    for k, on in ((0, on_plus), (1, on_minus)):
        v = jnp.broadcast_to(on[...].astype(jnp.float32)[:, None, :], (ST, FP, FP))
        v = jnp.sum(jnp.where(eye, v, 0.0), axis=2, keepdims=True)
        onset[k] = jnp.broadcast_to(v.reshape(ST * FP, 1), (ST * FP, LN))

    def first(i, _):
        at = pl.ds(pl.multiple_of(i * STEP, STEP), STEP)
        spec[at] = to_spectrum(direct[at].reshape(ROWS, NT), into, spread)
        return 0

    lax.fori_loop(0, ST // STEP, first, 0)
    pl.semaphore_wait(barrier, len(peers))

    def pack_spec(ph):
        last = spec[:, 4 * LN :]
        parts = [last[8 * b : 8 * b + 8] for b in range(4)]
        for q in range(NX):
            piece[ph, q, 0:ST] = spec[:, q * LN : (q + 1) * LN]
            piece[ph, q, ST : ST + 8] = pick(parts, q)

    def pack_bins(ph, blocks):
        parts = [blocks[4][8 * b : 8 * b + 8] for b in range(4)]
        for q in range(NX):
            piece[ph, q, 0:ST] = pick(blocks[:4], q)
            piece[ph, q, ST : ST + 8] = pick(parts, q)

    def exchange(ph):
        sent = []
        for o in (2, 1, 3):
            c = copy(("x", ph, o), piece.at[ph, freqs[o]], landed.at[ph, f], (freqs[o], src, rcv))
            c.start()
            sent.append(c)
        landed[ph, f] = piece[ph, f]
        for c in sent:
            c.wait()

    def take_spec(ph):
        for q in range(NX):
            spec[:, q * LN : (q + 1) * LN] = landed[ph, q, 0:ST]
        parts = [landed[ph, q, ST : ST + 8] for q in range(NX)]
        for b in range(4):
            spec[8 * b : 8 * b + 8, 4 * LN :] = pick(parts, b)

    def take_bins(ph):
        whole = [landed[ph, q, 0:ST] for q in range(NX)]
        parts = [landed[ph, q, ST : ST + 8] for q in range(NX)]
        out = [pick(whole, j) for j in range(4)]
        out.append(jnp.concatenate([pick(parts, b) for b in range(4)], axis=0))
        return out

    other = 1 - line
    own_rows = rows_at(line, 0)
    my_chunk = rcv_rows(high_y, core)
    opp_chunk = rcv_rows(1 - high_y, core)

    def gather_sources():
        pending = []

        def go(name, bins, at, device):
            c = copy(name, xs.at[bins, at], xs.at[bins, at], device)
            c.start()
            pending.append(c)
            return c

        whole, low, top = slice(0, BL), slice(0, ZA), slice(ZA, BL)
        cross = go(("gy", 0, 1), top, own_rows, across)
        cross_all = [go(("gy", 0, 0), low, own_rows, across)]
        ways = ((0, 1, right), (1, -1, left))
        moving = [None, None]
        moving_other = [None, None]
        for w, sign, dev in ways:
            moving[w] = go(("gz", w, 1), whole, own_rows, dev)
        cross.wait_recv()
        for w, sign, dev in ways:
            moving_other[w] = go(("gp", w, 1), top, rows_at(other, 0), dev)
        for hop in range(1, 4):
            for w, sign, dev in ways:
                moving[w].wait_recv()
                dist = -sign * hop
                at = rows_at(line, dist) if hop < 3 else half_at(line, dist, w)
                full = rows_at(line, dist)
                moving[w] = go(("gz", w, hop + 1), whole, at, dev)
                cross_all.append(go(("gy", dist, 0), low, full, across))
            for w, sign, dev in ways:
                moving_other[w].wait_recv()
                dist = -sign * hop
                at = rows_at(other, dist) if hop < 3 else half_at(other, dist, w)
                moving_other[w] = go(("gp", w, hop + 1), top, at, dev)
        for w in (0, 1):
            moving[w].wait_recv()
        cross_all.append(go(("gy", 4, 0), low, rows_at(line, 4), across))
        for w in (0, 1):
            moving_other[w].wait_recv()
        for c in cross_all:
            c.wait_recv()
        for c in pending:
            c.wait_send()

    def scatter_receivers():
        whole, low, top = slice(0, BL), slice(0, ZA), slice(ZA, BL)
        pending = []

        def go(name, source, target, device):
            c = copy(name, source, target, device)
            c.start()
            pending.append(c)
            return c

        cross = {}
        for dist in (4, 3, -3, 2, -2, 1, -1, 0):
            cross[dist] = go(
                ("sy", dist), h.at[low, rows_at(other, dist)], rsy.at[:, dist + 3], across
            )
        ways = ((0, 1, right), (1, -1, left))
        moving = [None, None]
        moving_other = [None, None]
        for w, sign, dev in ways:
            at = half_at(other, 4, w)
            moving_other[w] = go(
                ("sp", w, 4), h.at[top, at], rsp.at[w, 3, :, pl.ds(w * (ST // 2), ST // 2)], dev
            )
        cross[4].wait_recv()
        at = rows_at(line, 4)
        h[low, at] = h[low, at] + rsy[:, 7]
        for w, sign, dev in ways:
            at = half_at(line, 4, w)
            moving[w] = go(
                ("sz", w, 4), h.at[whole, at], rsz.at[w, 3, :, pl.ds(w * (ST // 2), ST // 2)], dev
            )
        for hop in (3, 2, 1):
            for w, sign, dev in ways:
                dist = sign * hop
                at = rows_at(line, dist)
                oat = rows_at(other, dist)
                cross[dist].wait_recv()
                h[low, at] = h[low, at] + rsy[:, dist + 3]
                moving[w].wait_recv()
                moving_other[w].wait_recv()
                if hop == 3:
                    part = slice(w * (ST // 2), (w + 1) * (ST // 2))
                    half = half_at(line, dist, w)
                    ohalf = half_at(other, dist, w)
                    h[:, half] = h[:, half] + rsz[w, 3, :, part]
                    h[top, ohalf] = h[top, ohalf] + rsp[w, 3, :, part]
                else:
                    h[:, at] = h[:, at] + rsz[w, hop]
                    h[top, oat] = h[top, oat] + rsp[w, hop]
                moving[w] = go(("sz", w, hop), h.at[whole, at], rsz.at[w, hop - 1], dev)
                moving_other[w] = go(("sp", w, hop), h.at[top, oat], rsp.at[w, hop - 1], dev)
        oat = rows_at(other, 0)
        for w in (0, 1):
            moving_other[w].wait_recv()
        h[top, oat] = h[top, oat] + rsp[0, 0] + rsp[1, 0]
        last = go(("sf", 0), h.at[top, oat], rsf, across)
        cross[0].wait_recv()
        h[low, own_rows] = h[low, own_rows] + rsy[:, 3]
        for w in (0, 1):
            moving[w].wait_recv()
        h[:, own_rows] = h[:, own_rows] + rsz[0, 0] + rsz[1, 0]
        last.wait_recv()
        h[top, own_rows] = h[top, own_rows] + rsf[...]
        for c in pending:
            c.wait_send()

    def iterate(it, _):
        pack_spec(0)
        exchange(0)
        for j, block in enumerate(take_bins(0)):
            xs[j, own_rows] = block
        gather_sources()

        def forward(j, _):
            x_high, x_low = halves(xs[j])
            both = mm(r_high[j], jnp.concatenate([x_high, x_low], axis=1))
            g = both[:, :LN] + both[:, LN:] + mm(r_low[j], x_high)
            real = is_real((SRC, LN))
            turned = swap_parts(g[SRC:], real)
            y[j] = g[:SRC] + jnp.where(real, -turned, turned)
            return 0

        lax.fori_loop(0, BL, forward, 0)

        sib = 1 - core
        a = copy(("ra", 0), y.at[:, rcv_rows(1 - high_y, sib)], r4a.at[0], sibling)
        a.start()
        b = copy(("ra", 1), y.at[:, rcv_rows(high_y, sib)], r4a.at[1], sibling)
        b.start()
        a.wait_recv()
        y[:, opp_chunk] = y[:, opp_chunk] + r4a[0]
        c = copy(("rb", 0), y.at[:, opp_chunk], r4b, opposite)
        c.start()
        b.wait_recv()
        y[:, my_chunk] = y[:, my_chunk] + r4a[1]
        c.wait_recv()
        total = y[:, my_chunk] + r4b[...]
        pack_bins(1, [total[j] for j in range(BL)])
        for d in (a, b, c):
            d.wait_send()
        exchange(1)
        take_spec(1)

        def up(i, _):
            at = pl.ds(pl.multiple_of(i * STEP, STEP), STEP)
            rows = pl.ds(pl.multiple_of(i * ROWS, ROWS), ROWS)
            t = lax.broadcasted_iota(jnp.int32, (ROWS, NT), 1).astype(jnp.float32)
            x = to_time(spec[at], collect, back)
            x = jnp.where(t < onset[1, rows, 0:1], x, 0.0)
            out_minus[at] = x.reshape(STEP, FP, NT)
            spec[at] = to_spectrum(x, into, spread)
            return 0

        lax.fori_loop(0, ST // STEP, up, 0)
        pack_spec(2)
        exchange(2)
        for j, block in enumerate(take_bins(2)):
            cs[j, my_chunk] = block
        a = copy(("ca", 0), cs.at[:, my_chunk], cs.at[:, my_chunk], opposite)
        a.start()
        b = copy(("ca", 1), cs.at[:, my_chunk], cs.at[:, my_chunk], sibling)
        b.start()
        a.wait_recv()
        c = copy(("ca", 2), cs.at[:, opp_chunk], cs.at[:, opp_chunk], sibling)
        c.start()
        b.wait_recv()
        c.wait_recv()
        for d in (a, b, c):
            d.wait_send()

        def adjoint(j, _):
            real = is_real((SRC, LN))
            block = cs[j]
            turned = swap_parts(block, real)
            stacked = jnp.concatenate([block, jnp.where(real, turned, -turned)], axis=0)
            c_high, c_low = halves(stacked)
            both = mm(t_high[j], jnp.concatenate([c_high, c_low], axis=1))
            h[j] = both[:, :LN] + both[:, LN:] + mm(t_low[j], c_high)
            return 0

        lax.fori_loop(0, BL, adjoint, 0)
        scatter_receivers()
        pack_bins(3, [h[j, own_rows] for j in range(BL)])
        exchange(3)
        take_spec(3)

        def down(i, _):
            at = pl.ds(pl.multiple_of(i * STEP, STEP), STEP)
            rows = pl.ds(pl.multiple_of(i * ROWS, ROWS), ROWS)
            t = lax.broadcasted_iota(jnp.int32, (ROWS, NT), 1).astype(jnp.float32)
            x = to_time(spec[at], collect, back)
            x = direct[at].reshape(ROWS, NT) + jnp.where(t < onset[0, rows, 0:1], x, 0.0)
            out_plus[at] = x.reshape(STEP, FP, NT)

            @pl.when(it < ITERS - 1)
            def _():
                spec[at] = to_spectrum(x, into, spread)

            return 0

        lax.fori_loop(0, ST // STEP, down, 0)
        return 0

    lax.fori_loop(0, ITERS, iterate, 0)


MESSAGES = 96


def per_device(direct, reflection, onset_plus, onset_minus):
    vmem = pl.BlockSpec(memory_space=pltpu.VMEM)
    f32, bf16 = jnp.float32, jnp.bfloat16
    traces = jax.ShapeDtypeStruct((ST, FP, NT), f32)
    return pl.pallas_call(
        kernel,
        out_shape=(traces, traces),
        in_specs=[vmem] * 8,
        out_specs=(vmem, vmem),
        scratch_shapes=[
            pltpu.VMEM((BL, 2 * SRC, RCV), bf16),
            pltpu.VMEM((BL, 2 * SRC, RCV), bf16),
            pltpu.VMEM((BL, RCV, 2 * SRC), bf16),
            pltpu.VMEM((BL, RCV, 2 * SRC), bf16),
            pltpu.VMEM((2, ST * FP, LN), f32),
            pltpu.VMEM((ST, WIDE), f32),
            pltpu.VMEM((4, NX, ST + 8, LN), f32),
            pltpu.VMEM((4, NX, ST + 8, LN), f32),
            pltpu.VMEM((BL, RCV, LN), f32),
            pltpu.VMEM((BL, SRC, LN), f32),
            pltpu.VMEM((2, BL, ST, LN), f32),
            pltpu.VMEM((BL, ST, LN), f32),
            pltpu.VMEM((BL, SRC, LN), f32),
            pltpu.VMEM((BL, RCV, LN), f32),
            pltpu.VMEM((ZA, NZ, ST, LN), f32),
            pltpu.VMEM((2, 4, BL, ST, LN), f32),
            pltpu.VMEM((2, 4, BL - ZA, ST, LN), f32),
            pltpu.VMEM((BL - ZA, ST, LN), f32),
            pltpu.SemaphoreType.DMA((MESSAGES,)),
            pltpu.SemaphoreType.DMA((MESSAGES,)),
        ],
        compiler_params=pltpu.CompilerParams(
            collective_id=0, has_side_effects=True, vmem_limit_bytes=56 * 1024 * 1024
        ),
    )(direct, reflection, onset_plus, onset_minus, *[jnp.asarray(a) for a in tables()])


def solution(mesh):
    in_specs = (
        P(("rcv", "src"), "freq", None),
        P(None, "freq", "src", "rcv"),
        P(("rcv", "src"), "freq"),
        P(("src", "rcv"), "freq"),
    )
    out_specs = (P(("rcv", "src"), "freq", None), P(("src", "rcv"), "freq", None))
    return jax.shard_map(
        per_device, mesh=mesh, in_specs=in_specs, out_specs=out_specs, check_vma=False
    )
```

```python
import math

import jax
import jax.numpy as jnp
import ml_dtypes
import numpy as np
from jax import lax
from jax.experimental import pallas as pl
from jax.experimental.pallas import tpu as pltpu
from jax.sharding import PartitionSpec as P

FIRST_BIN = 32
ITERS = 2
MESH = pl.DeviceIdType.MESH

NF = 20
NX = 4
BL = NF // NX
FP = 16
GROUPS = 2
SH = GROUPS
PG = FP // GROUPS
ST = 32 // SH
NT = 1024
NZ = 8
LN = 128
SRC = 128
RCV = 512
NS = 16
NR = 4
PR = ST + 8
COLS = 2 * NF
WIDE = COLS * FP
STEP = 8
ROWS = STEP * FP


def tables():
    k = (np.arange(NT)[:, None] * (FIRST_BIN + np.arange(NF))[None, :]) % NT
    angle = 2.0 * math.pi * k / NT
    scale = math.sqrt(2.0 / NT)
    table = np.stack([scale * np.cos(angle), -scale * np.sin(angle)], axis=2)
    table = table.reshape(NT, COLS).astype(np.float32)
    high = table.astype(ml_dtypes.bfloat16).astype(np.float32)
    low = (table - high).astype(ml_dtypes.bfloat16).astype(np.float32)
    into = np.zeros((2, NT, LN), np.float32)
    into[0, :, :COLS] = high
    into[0, :, COLS : 2 * COLS] = low
    into[1, :, :COLS] = high
    back = np.zeros((LN, NT), np.float32)
    back[:COLS] = high.T
    back[COLS : 2 * COLS] = high.T
    back[2 * COLS : 3 * COLS] = low.T
    spread = np.zeros((LN, WIDE), np.float32)
    collect = np.zeros((2, WIDE, LN), np.float32)
    for b in range(NF):
        for c in range(2):
            for p in range(FP):
                f, j = b // BL, b % BL
                lane = (f * LN + j * 32 if j < 4 else 4 * LN + f * 32) + c * FP + p
                col = 2 * b + c
                spread[col, lane] = 1
                spread[COLS + col, lane] = 1
                collect[0, lane, col] = 1
                collect[0, lane, 2 * COLS + col] = 1
                collect[1, lane, COLS + col] = 1
    return [a.astype(ml_dtypes.bfloat16) for a in (into, spread, collect, back)]


def halves(x):
    high = x.astype(jnp.bfloat16)
    return high, (x - high.astype(jnp.float32)).astype(jnp.bfloat16)


def mm(a, b):
    return lax.dot_general(a, b, (((1,), (0,)), ((), ())), preferred_element_type=jnp.float32)


def turn(x, lanes):
    lanes = lanes % LN
    return x if lanes == 0 else pltpu.roll(x, lanes, 1)


def pick(parts, i):
    group = lax.broadcasted_iota(jnp.int32, parts[0].shape, 1) // 32
    out = turn(parts[0], -i * 32)
    for k in range(1, len(parts)):
        out = jnp.where(group == k, turn(parts[k], (k - i) * 32), out)
    return out


def own_focus():
    row = lax.broadcasted_iota(jnp.int32, (ROWS, WIDE), 0) % FP
    lane = lax.broadcasted_iota(jnp.int32, (ROWS, WIDE), 1) % FP
    return row == lane


def to_spectrum(x, into, spread):
    high, low = halves(x)
    s = mm(high, into[0]) + mm(low, into[1])
    high, low = halves(s)
    e = mm(high, spread[...]) + mm(low, spread[...])
    e = jnp.where(own_focus(), e, 0.0).reshape(STEP, FP, WIDE)
    return jnp.sum(e, axis=1)


def to_time(z, collect, back):
    high = z.astype(jnp.bfloat16).astype(jnp.float32)
    low = z - high
    own = own_focus()

    def rows(v):
        v = jnp.broadcast_to(v[:, None, :], (STEP, FP, WIDE)).reshape(ROWS, WIDE)
        return jnp.where(own, v, 0.0).astype(jnp.bfloat16)

    g = mm(rows(high), collect[0]) + mm(rows(low), collect[1])
    return mm(g.astype(jnp.bfloat16), back[...])


def is_real(shape):
    return lax.broadcasted_iota(jnp.int32, shape, 1) % 32 < FP


def swap_parts(x, real):
    return jnp.where(real, turn(x, -FP), turn(x, FP))


def lane_block(shape):
    return lax.broadcasted_iota(jnp.int32, shape, 1) // PG % SH


def unfold(x):
    if SH == 1:
        return x
    at = lane_block(x.shape)
    return jnp.concatenate(
        [jnp.where(at == 0, x, turn(x, PG)), jnp.where(at == 1, x, turn(x, -PG))], axis=0
    )


def fold(x):
    if SH == 1:
        return x
    n = x.shape[0] // 2
    return jnp.where(lane_block((n, LN)) == 0, x[:n], x[n:])


def reorder(x, outer, inner):
    if SH == 1:
        return x
    return jnp.concatenate(
        [x[(o * SH + s) * inner : (o * SH + s + 1) * inner] for s in range(SH) for o in range(outer)],
        axis=0,
    )


def kernel(
    direct, refl, on_plus, on_minus, into, spread, collect, back,
    out_plus, out_minus,
    r_high, r_low, t_high, t_low, onset, spec, piece, piece_sum, land_g, land_r, land_f, land_s,
    xs, y, r4a, cs, h, rs, send_sem, recv_sem,
):
    f = lax.axis_index("freq")
    src = lax.axis_index("src")
    rcv = lax.axis_index("rcv")
    line = src // NZ
    z = src % NZ
    other = 1 - line
    high_y = rcv // 2
    core = rcv % 2
    freqs = [f] + [(f + o) % NX for o in range(1, NX)]

    def at_src(dl, dz, o=0):
        on = other if dl else line
        return (freqs[o], on * NZ + (z + dz + NZ) % NZ, rcv)

    def at_rcv(dh, dc, o=0):
        hy = 1 - high_y if dh else high_y
        return (freqs[o], src, hy * 2 + (1 - core if dc else core))

    near = [(0, 0), (1, 0), (0, 1), (0, -1), (0, 2), (0, -2)]
    peers = [at_src(*k, o) for k in near for o in range(NX) if k != (0, 0) or o]
    peers += [at_src(1, d) for d in (1, -1, 2, -2)]
    peers += [at_rcv(1, 0, o) for o in range(NX)] + [at_rcv(0, 1)]
    barrier = pltpu.get_barrier_semaphore()
    for peer in peers:
        pl.semaphore_signal(barrier, inc=1, device_id=peer, device_id_type=MESH)

    names = {}

    def copy(name, source, target, device):
        n = names.setdefault(name, len(names))
        return pltpu.make_async_remote_copy(
            src_ref=source, dst_ref=target, send_sem=send_sem.at[n], recv_sem=recv_sem.at[n],
            device_id=device, device_id_type=MESH,
        )

    def rows_at(dl, dz, part=None):
        block = (other if dl else line) * NZ + (z + dz + NZ) % NZ
        if part is None:
            return pl.ds(pl.multiple_of(block * ST, ST), ST)
        return pl.ds(pl.multiple_of(block * ST + part * (ST // 2), ST // 2), ST // 2)

    def rcv_rows(dh, dc):
        block = (1 - high_y if dh else high_y) * 2 + (1 - core if dc else core)
        return pl.ds(pl.multiple_of(block * ST, ST), ST)

    def prepare(j, _):
        block = reorder(refl[:, j].reshape(2 * SRC, RCV), 2 * NR, ST)
        block = reorder(block.T, NS, ST)
        high, low = halves(block)
        t_high[j] = high
        t_low[j] = low
        high, low = halves(block.T)
        r_high[j] = high
        r_low[j] = low
        return 0

    lax.fori_loop(0, BL, prepare, 0)
    whole = (ST * SH, FP, FP)
    eye = lax.broadcasted_iota(jnp.int32, whole, 1) == lax.broadcasted_iota(jnp.int32, whole, 2)
    for k, on in ((0, on_plus), (1, on_minus)):
        v = jnp.broadcast_to(on[...].astype(jnp.float32)[:, None, :], whole)
        v = jnp.sum(jnp.where(eye, v, 0.0), axis=2, keepdims=True)
        onset[k] = jnp.broadcast_to(v, (ST * SH, FP, LN))

    def load(ref, grp, i, lanes):
        parts = [
            ref[pl.ds(pl.multiple_of(s * ST + i * STEP, STEP), STEP), grp * PG : (grp + 1) * PG]
            for s in range(SH)
        ]
        x = parts[0] if SH == 1 else jnp.concatenate(parts, axis=1)
        return x.reshape(ROWS, lanes)

    def store(ref, grp, i, x):
        x = x.reshape(STEP, FP, NT)
        for s in range(SH):
            at = pl.ds(pl.multiple_of(s * ST + i * STEP, STEP), STEP)
            ref[at, grp * PG : (grp + 1) * PG] = x[:, s * PG : (s + 1) * PG]

    def keep(k, grp, i):
        t = lax.broadcasted_iota(jnp.int32, (ROWS, NT), 1).astype(jnp.float32)
        return t < load(onset.at[k], grp, i, LN)[:, 0:1]

    parts_of = ST // 8

    def pack_spec(grp):
        last = spec[grp, :, 4 * LN :]
        parts = [last[8 * b : 8 * b + 8] for b in range(parts_of)]
        for q in range(NX):
            piece[grp, q, 0:ST] = spec[grp, :, q * LN : (q + 1) * LN]
            piece[grp, q, ST : ST + 8] = pick(parts, q)

    def pack_bins(grp, n, blocks):
        parts = [blocks[4][8 * b : 8 * b + 8] for b in range(parts_of)]
        for q in range(NX):
            piece_sum[grp, n, q, 0:ST] = pick(blocks[:4], q)
            piece_sum[grp, n, q, ST : ST + 8] = pick(parts, q)

    def take_spec(grp, pieces):
        for q in range(NX):
            spec[grp, :, q * LN : (q + 1) * LN] = pieces[q][0:ST]
        parts = [pieces[q][ST : ST + 8] for q in range(NX)]
        for b in range(parts_of):
            spec[grp, 8 * b : 8 * b + 8, 4 * LN :] = pick(parts, b)

    def take_bins(pieces):
        full = [p[0:ST] for p in pieces]
        parts = [p[ST : ST + 8] for p in pieces]
        out = [pick(full, j) for j in range(4)]
        out.append(jnp.concatenate([pick(parts, b) for b in range(parts_of)], axis=0))
        return out

    def program(grp):
        def go(name, source, target, device):
            c = copy((grp,) + name, source, target, device)
            c.start()
            return c

        def spectrum_of(i, _):
            at = pl.ds(pl.multiple_of(i * STEP, STEP), STEP)
            spec[grp, at] = to_spectrum(load(direct, grp, i, NT), into, spread)
            return 0

        lax.fori_loop(0, ST // STEP, spectrum_of, 0)
        if grp == 0:
            pl.semaphore_wait(barrier, len(peers))

        for it in range(ITERS):
            pack_spec(grp)
            sent = []
            stage = {}
            for n in (4, 5, 2, 3, 1, 0):
                for o in (2, 1, 3, 0):
                    if n or o:
                        c = go(
                            ("g", n, o), piece.at[grp, freqs[o]], land_g.at[grp, n, f],
                            at_src(*near[n], o),
                        )
                        stage.setdefault(n, []).append(c)
                        sent.append(c)
            land_g[grp, 0, f] = piece[grp, f]
            late = []

            def arrive(n):
                for c in stage[n]:
                    c.wait_recv()
                dl, dz = near[n]
                at = rows_at(dl, -dz)
                blocks = take_bins([land_g[grp, n, q] for q in range(NX)])
                for j in range(BL):
                    xs[grp, j, at] = blocks[j]
                return at

            def forward_to(name, at, dl, dz):
                c = go(name, xs.at[grp, :, at], xs.at[grp, :, at], at_src(dl, dz))
                late.append(c)
                sent.append(c)

            yield
            for n in (2, 3):
                at = arrive(n)
                forward_to(("gy", n), at, 1, 0)
            yield
            for n, w, way in ((4, 0, 1), (5, 1, -1)):
                at = arrive(n)
                half = rows_at(0, -2 * way, w)
                forward_to(("gd", n), at, 1, way)
                forward_to(("g3", n), at, 0, way)
                forward_to(("ge", n), half, 1, 2 * way)
                forward_to(("g4", n), half, 0, 2 * way)
                forward_to(("gy", n), at, 1, 0)
            arrive(0)
            arrive(1)
            yield
            for c in late:
                c.wait_recv()
            for c in sent:
                c.wait_send()

            def forward(j, _):
                x_high, x_low = halves(unfold(xs[grp, j]))
                both = mm(r_high[j], jnp.concatenate([x_high, x_low], axis=1))
                g = fold(both[:, :LN] + both[:, LN:] + mm(r_low[j], x_high))
                n = SRC // SH
                real = is_real((n, LN))
                turned = swap_parts(g[n:], real)
                y[grp, j] = g[:n] + jnp.where(real, -turned, turned)
                return 0

            lax.fori_loop(0, BL, forward, 0)

            pair = [
                go(("ra", dh), y.at[grp, :, rcv_rows(dh, 1)], r4a.at[grp, dh], at_rcv(0, 1))
                for dh in (1, 0)
            ]
            yield
            sent = list(pair)
            stage = []
            for dh, c in zip((1, 0), pair):
                c.wait_recv()
                total = y[grp, :, rcv_rows(dh, 0)] + r4a[grp, dh]
                pack_bins(grp, dh, [total[j] for j in range(BL)])
                for o in (2, 1, 3, 0):
                    if dh or o:
                        stage.append(
                            go(
                                ("rx", dh, o), piece_sum.at[grp, dh, freqs[o]],
                                land_r.at[grp, dh, f], at_rcv(dh, 0, o),
                            )
                        )
            land_r[grp, 0, f] = piece_sum[grp, 0, f]
            yield
            for c in stage:
                c.wait_recv()
            for c in sent + stage:
                c.wait_send()
            take_spec(grp, [land_r[grp, 0, q] + land_r[grp, 1, q] for q in range(NX)])

            def up(i, _):
                at = pl.ds(pl.multiple_of(i * STEP, STEP), STEP)
                x = jnp.where(keep(1, grp, i), to_time(spec[grp, at], collect, back), 0.0)
                store(out_minus, grp, i, x)
                spec[grp, at] = to_spectrum(x, into, spread)
                return 0

            lax.fori_loop(0, ST // STEP, up, 0)

            pack_spec(grp)
            stage = [[], []]
            for dh in (1, 0):
                for o in (2, 1, 3, 0):
                    if dh or o:
                        stage[dh].append(
                            go(
                                ("cx", dh, o), piece.at[grp, freqs[o]], land_f.at[grp, dh, f],
                                at_rcv(dh, 0, o),
                            )
                        )
            land_f[grp, 0, f] = piece[grp, f]
            yield
            pair = []
            for dh in (0, 1):
                for c in stage[dh]:
                    c.wait_recv()
                at = rcv_rows(dh, 0)
                blocks = take_bins([land_f[grp, dh, q] for q in range(NX)])
                for j in range(BL):
                    cs[grp, j, at] = blocks[j]
                pair.append(go(("cc", dh), cs.at[grp, :, at], cs.at[grp, :, at], at_rcv(0, 1)))
            yield
            for c in pair:
                c.wait_recv()
            for c in pair + stage[0] + stage[1]:
                c.wait_send()

            def adjoint(j, _):
                block = cs[grp, j]
                real = is_real(block.shape)
                turned = swap_parts(block, real)
                both = jnp.concatenate([block, jnp.where(real, turned, -turned)], axis=0)
                c_high, c_low = halves(unfold(both))
                both = mm(t_high[j], jnp.concatenate([c_high, c_low], axis=1))
                h[grp, j] = fold(both[:, :LN] + both[:, LN:] + mm(t_low[j], c_high))
                return 0

            lax.fori_loop(0, BL, adjoint, 0)

            sent = []
            stage = {}

            def part_to(name, slot, dl, dist, dest, part=None):
                target = rs.at[grp, slot]
                if part is not None:
                    target = rs.at[grp, slot, :, pl.ds(part * (ST // 2), ST // 2)]
                c = go(name, h.at[grp, :, rows_at(dl, dist, part)], target, at_src(*dest))
                stage[slot] = stage.get(slot, []) + [c]
                sent.append(c)

            for w, way in ((0, 1), (1, -1)):
                part_to(("se", w), 8 + w, 1, 4, (1, 2 * way), w)
                part_to(("s4", w), 6 + w, 0, 4, (0, 2 * way), w)
                part_to(("sd", w), 4 + w, 1, 3 * way, (1, way))
                part_to(("s3", w), 2 + w, 0, 3 * way, (0, way))
            for w, way in ((0, 1), (1, -1)):
                part_to(("sy", 2, w), 10 + w, 1, 2 * way, (1, 0))
            for w, way in ((0, 1), (1, -1)):
                part_to(("sy", 1, w), w, 1, way, (1, 0))

            last = {}

            def finish(n, blocks):
                pack_bins(grp, n, blocks)
                for o in (2, 1, 3, 0):
                    if n or o:
                        c = go(
                            ("sx", n, o), piece_sum.at[grp, n, freqs[o]], land_s.at[grp, n, f],
                            at_src(*near[n], o),
                        )
                        last.setdefault(n, []).append(c)
                        sent.append(c)

            def bins_of(total):
                return [total[j] for j in range(BL)]

            finish(1, [h[grp, j, rows_at(1, 0)] for j in range(BL)])
            finish(0, [h[grp, j, rows_at(0, 0)] for j in range(BL)])
            land_s[grp, 0, f] = piece_sum[grp, 0, f]
            yield
            for w, way in ((0, 1), (1, -1)):
                for c in stage[w]:
                    c.wait_recv()
                finish(2 + w, bins_of(h[grp, :, rows_at(0, way)] + rs[grp, w]))
            yield
            for w, way in ((0, 1), (1, -1)):
                for slot in (2 + w, 4 + w, 6 + w, 8 + w, 10 + w):
                    for c in stage[slot]:
                        c.wait_recv()
                total = h[grp, :, rows_at(0, 2 * way)] + rs[grp, 2 + w] + rs[grp, 4 + w]
                total = total + rs[grp, 10 + w]
                half = slice(w * (ST // 2), (w + 1) * (ST // 2))
                four = rs[grp, 6 + w, :, half] + rs[grp, 8 + w, :, half]
                some = [total[:, :8], total[:, 8:]] if ST == 16 else [total[:, :16], total[:, 16:]]
                some[w] = some[w] + four
                finish(4 + w, bins_of(jnp.concatenate(some, axis=1)))
            yield
            for n in range(6):
                for c in last[n]:
                    c.wait_recv()
            for c in sent:
                c.wait_send()
            pieces = []
            for q in range(NX):
                total = land_s[grp, 0, q]
                for n in range(1, 6):
                    total = total + land_s[grp, n, q]
                pieces.append(total)
            take_spec(grp, pieces)

            def down(i, _):
                at = pl.ds(pl.multiple_of(i * STEP, STEP), STEP)
                x = jnp.where(keep(0, grp, i), to_time(spec[grp, at], collect, back), 0.0)
                x = load(direct, grp, i, NT) + x
                if it < ITERS - 1:
                    spec[grp, at] = to_spectrum(x, into, spread)
                else:
                    store(out_plus, grp, i, x)
                return 0

            lax.fori_loop(0, ST // STEP, down, 0)

    running = [program(grp) for grp in range(GROUPS)]
    while running:
        for p in list(running):
            if next(p, 0) == 0:
                running.remove(p)


MESSAGES = 88 * GROUPS


def per_device(direct, reflection, onset_plus, onset_minus):
    vmem = pl.BlockSpec(memory_space=pltpu.VMEM)
    f32, bf16 = jnp.float32, jnp.bfloat16
    traces = jax.ShapeDtypeStruct((ST * SH, FP, NT), f32)
    return pl.pallas_call(
        kernel,
        out_shape=(traces, traces),
        in_specs=[vmem] * 8,
        out_specs=(vmem, vmem),
        scratch_shapes=[
            pltpu.VMEM((BL, 2 * SRC, RCV), bf16),
            pltpu.VMEM((BL, 2 * SRC, RCV), bf16),
            pltpu.VMEM((BL, RCV, 2 * SRC), bf16),
            pltpu.VMEM((BL, RCV, 2 * SRC), bf16),
            pltpu.VMEM((2, ST * SH, FP, LN), f32),
            pltpu.VMEM((GROUPS, ST, WIDE), f32),
            pltpu.VMEM((GROUPS, NX, PR, LN), f32),
            pltpu.VMEM((GROUPS, 6, NX, PR, LN), f32),
            pltpu.VMEM((GROUPS, 6, NX, PR, LN), f32),
            pltpu.VMEM((GROUPS, 2, NX, PR, LN), f32),
            pltpu.VMEM((GROUPS, 2, NX, PR, LN), f32),
            pltpu.VMEM((GROUPS, 6, NX, PR, LN), f32),
            pltpu.VMEM((GROUPS, BL, NS * ST, LN), f32),
            pltpu.VMEM((GROUPS, BL, NR * ST, LN), f32),
            pltpu.VMEM((GROUPS, 2, BL, ST, LN), f32),
            pltpu.VMEM((GROUPS, BL, NR * ST, LN), f32),
            pltpu.VMEM((GROUPS, BL, NS * ST, LN), f32),
            pltpu.VMEM((GROUPS, 12, BL, ST, LN), f32),
            pltpu.SemaphoreType.DMA((MESSAGES,)),
            pltpu.SemaphoreType.DMA((MESSAGES,)),
        ],
        compiler_params=pltpu.CompilerParams(
            collective_id=0, has_side_effects=True, vmem_limit_bytes=56 * 1024 * 1024
        ),
    )(direct, reflection, onset_plus, onset_minus, *[jnp.asarray(a) for a in tables()])


def solution(mesh):
    in_specs = (
        P(("rcv", "src"), "freq", None),
        P(None, "freq", "src", "rcv"),
        P(("rcv", "src"), "freq"),
        P(("src", "rcv"), "freq"),
    )
    out_specs = (P(("rcv", "src"), "freq", None), P(("src", "rcv"), "freq", None))
    return jax.shard_map(
        per_device, mesh=mesh, in_specs=in_specs, out_specs=out_specs, check_vma=False
    )
```

```python
import math

import jax
import jax.numpy as jnp
import ml_dtypes
import numpy as np
from jax import lax
from jax.experimental import pallas as pl
from jax.experimental.pallas import tpu as pltpu
from jax.sharding import PartitionSpec as P

FIRST_BIN = 32
ITERS = 2
MESH = pl.DeviceIdType.MESH

NF = 20
NX = 4
BL = NF // NX
FP = 16
GROUPS = 2
SH = GROUPS
PG = FP // GROUPS
ST = 32 // SH
NT = 1024
NZ = 8
LN = 128
SRC = 128
RCV = 512
NS = 16
NR = 4
PR = ST + 8
COLS = 2 * NF
WIDE = COLS * FP
STEP = 8
ROWS = STEP * FP


def tables():
    k = (np.arange(NT)[:, None] * (FIRST_BIN + np.arange(NF))[None, :]) % NT
    angle = 2.0 * math.pi * k / NT
    scale = math.sqrt(2.0 / NT)
    table = np.stack([scale * np.cos(angle), -scale * np.sin(angle)], axis=2)
    table = table.reshape(NT, COLS).astype(np.float32)
    high = table.astype(ml_dtypes.bfloat16).astype(np.float32)
    low = (table - high).astype(ml_dtypes.bfloat16).astype(np.float32)
    into = np.zeros((2, NT, LN), np.float32)
    into[0, :, :COLS] = high
    into[0, :, COLS : 2 * COLS] = low
    into[1, :, :COLS] = high
    back = np.zeros((LN, NT), np.float32)
    back[:COLS] = high.T
    back[COLS : 2 * COLS] = high.T
    back[2 * COLS : 3 * COLS] = low.T
    spread = np.zeros((LN, WIDE), np.float32)
    collect = np.zeros((2, WIDE, LN), np.float32)
    for b in range(NF):
        for c in range(2):
            for p in range(FP):
                f, j = b // BL, b % BL
                lane = (f * LN + j * 32 if j < 4 else 4 * LN + f * 32) + c * FP + p
                col = 2 * b + c
                spread[col, lane] = 1
                spread[COLS + col, lane] = 1
                collect[0, lane, col] = 1
                collect[0, lane, 2 * COLS + col] = 1
                collect[1, lane, COLS + col] = 1
    return [a.astype(ml_dtypes.bfloat16) for a in (into, spread, collect, back)]


def halves(x):
    high = x.astype(jnp.bfloat16)
    return high, (x - high.astype(jnp.float32)).astype(jnp.bfloat16)


def mm(a, b):
    return lax.dot_general(a, b, (((1,), (0,)), ((), ())), preferred_element_type=jnp.float32)


def turn(x, lanes):
    lanes = lanes % LN
    return x if lanes == 0 else pltpu.roll(x, lanes, 1)


def pick(parts, i):
    group = lax.broadcasted_iota(jnp.int32, parts[0].shape, 1) // 32
    out = turn(parts[0], -i * 32)
    for k in range(1, len(parts)):
        out = jnp.where(group == k, turn(parts[k], (k - i) * 32), out)
    return out


def own_focus():
    row = lax.broadcasted_iota(jnp.int32, (ROWS, WIDE), 0) % FP
    lane = lax.broadcasted_iota(jnp.int32, (ROWS, WIDE), 1) % FP
    return row == lane


def to_spectrum(x, into, spread):
    high, low = halves(x)
    s = mm(high, into[0]) + mm(low, into[1])
    high, low = halves(s)
    e = mm(high, spread[...]) + mm(low, spread[...])
    e = jnp.where(own_focus(), e, 0.0).reshape(STEP, FP, WIDE)
    return jnp.sum(e, axis=1)


def to_time(z, collect, back):
    high = z.astype(jnp.bfloat16).astype(jnp.float32)
    low = z - high
    own = own_focus()

    def rows(v):
        v = jnp.broadcast_to(v[:, None, :], (STEP, FP, WIDE)).reshape(ROWS, WIDE)
        return jnp.where(own, v, 0.0).astype(jnp.bfloat16)

    g = mm(rows(high), collect[0]) + mm(rows(low), collect[1])
    return mm(g.astype(jnp.bfloat16), back[...])


def is_real(shape):
    return lax.broadcasted_iota(jnp.int32, shape, 1) % 32 < FP


def swap_parts(x, real):
    return jnp.where(real, turn(x, -FP), turn(x, FP))


def lane_block(shape):
    return lax.broadcasted_iota(jnp.int32, shape, 1) // PG % SH


def unfold(x):
    if SH == 1:
        return x
    at = lane_block(x.shape)
    return jnp.concatenate(
        [jnp.where(at == 0, x, turn(x, PG)), jnp.where(at == 1, x, turn(x, -PG))], axis=0
    )


def fold(x):
    if SH == 1:
        return x
    n = x.shape[0] // 2
    return jnp.where(lane_block((n, LN)) == 0, x[:n], x[n:])


def reorder(x, outer, inner):
    if SH == 1:
        return x
    return jnp.concatenate(
        [x[(o * SH + s) * inner : (o * SH + s + 1) * inner] for s in range(SH) for o in range(outer)],
        axis=0,
    )


def kernel(
    direct, refl, on_plus, on_minus, into, spread, collect, back,
    out_plus, out_minus,
    r_high, r_low, t_high, t_low, onset, spec, piece, piece_sum, land_g, land_r, land_f, land_s,
    xs, y, r4a, cs, h, rs, send_sem, recv_sem,
):
    f = lax.axis_index("freq")
    src = lax.axis_index("src")
    rcv = lax.axis_index("rcv")
    line = src // NZ
    z = src % NZ
    other = 1 - line
    high_y = rcv // 2
    core = rcv % 2
    freqs = [f] + [(f + o) % NX for o in range(1, NX)]

    def at_src(dl, dz, o=0):
        on = other if dl else line
        return (freqs[o], on * NZ + (z + dz + NZ) % NZ, rcv)

    def at_rcv(dh, dc, o=0):
        hy = 1 - high_y if dh else high_y
        return (freqs[o], src, hy * 2 + (1 - core if dc else core))

    near = [(0, 0), (1, 0), (0, 1), (0, -1), (0, 2), (0, -2)]
    peers = [at_src(*k, o) for k in near for o in range(NX) if k != (0, 0) or o]
    peers += [at_src(1, d) for d in (1, -1, 2, -2)]
    peers += [at_rcv(1, 0, o) for o in range(NX)] + [at_rcv(0, 1)]
    barrier = pltpu.get_barrier_semaphore()
    for peer in peers:
        pl.semaphore_signal(barrier, inc=1, device_id=peer, device_id_type=MESH)

    names = {}

    def copy(name, source, target, device):
        n = names.setdefault(name, len(names))
        return pltpu.make_async_remote_copy(
            src_ref=source, dst_ref=target, send_sem=send_sem.at[n], recv_sem=recv_sem.at[n],
            device_id=device, device_id_type=MESH,
        )

    def rows_at(dl, dz, part=None):
        block = (other if dl else line) * NZ + (z + dz + NZ) % NZ
        if part is None:
            return pl.ds(pl.multiple_of(block * ST, ST), ST)
        return pl.ds(pl.multiple_of(block * ST + part * (ST // 2), ST // 2), ST // 2)

    def rcv_rows(dh, dc):
        block = (1 - high_y if dh else high_y) * 2 + (1 - core if dc else core)
        return pl.ds(pl.multiple_of(block * ST, ST), ST)

    def prepare(j, _):
        block = reorder(refl[:, j].reshape(2 * SRC, RCV), 2 * NR, ST)
        block = reorder(block.T, NS, ST)
        high, low = halves(block)
        t_high[j] = high
        t_low[j] = low
        high, low = halves(block.T)
        r_high[j] = high
        r_low[j] = low
        return 0

    lax.fori_loop(0, BL, prepare, 0)
    whole = (ST * SH, FP, FP)
    eye = lax.broadcasted_iota(jnp.int32, whole, 1) == lax.broadcasted_iota(jnp.int32, whole, 2)
    for k, on in ((0, on_plus), (1, on_minus)):
        v = jnp.broadcast_to(on[...].astype(jnp.float32).T[:, None, :], whole)
        v = jnp.sum(jnp.where(eye, v, 0.0), axis=2, keepdims=True)
        onset[k] = jnp.broadcast_to(v, (ST * SH, FP, LN))

    def load(ref, grp, i, lanes):
        parts = [
            ref[pl.ds(pl.multiple_of(s * ST + i * STEP, STEP), STEP), grp * PG : (grp + 1) * PG]
            for s in range(SH)
        ]
        x = parts[0] if SH == 1 else jnp.concatenate(parts, axis=1)
        return x.reshape(ROWS, lanes)

    def store(ref, grp, i, x):
        x = x.reshape(STEP, FP, NT)
        for s in range(SH):
            at = pl.ds(pl.multiple_of(s * ST + i * STEP, STEP), STEP)
            ref[at, grp * PG : (grp + 1) * PG] = x[:, s * PG : (s + 1) * PG]

    def keep(k, grp, i):
        t = lax.broadcasted_iota(jnp.int32, (ROWS, NT), 1).astype(jnp.float32)
        return t < load(onset.at[k], grp, i, LN)[:, 0:1]

    parts_of = ST // 8

    def pack_spec(grp):
        last = spec[grp, :, 4 * LN :]
        parts = [last[8 * b : 8 * b + 8] for b in range(parts_of)]
        for q in range(NX):
            piece[grp, q, 0:ST] = spec[grp, :, q * LN : (q + 1) * LN]
            piece[grp, q, ST : ST + 8] = pick(parts, q)

    def pack_bins(grp, n, blocks):
        parts = [blocks[4][8 * b : 8 * b + 8] for b in range(parts_of)]
        for q in range(NX):
            piece_sum[grp, n, q, 0:ST] = pick(blocks[:4], q)
            piece_sum[grp, n, q, ST : ST + 8] = pick(parts, q)

    def take_spec(grp, pieces):
        for q in range(NX):
            spec[grp, :, q * LN : (q + 1) * LN] = pieces[q][0:ST]
        parts = [pieces[q][ST : ST + 8] for q in range(NX)]
        for b in range(parts_of):
            spec[grp, 8 * b : 8 * b + 8, 4 * LN :] = pick(parts, b)

    def take_bins(pieces):
        full = [p[0:ST] for p in pieces]
        parts = [p[ST : ST + 8] for p in pieces]
        out = [pick(full, j) for j in range(4)]
        out.append(jnp.concatenate([pick(parts, b) for b in range(parts_of)], axis=0))
        return out

    def program(grp):
        def go(name, source, target, device):
            c = copy((grp,) + name, source, target, device)
            c.start()
            return c

        def spectrum_of(i, _):
            at = pl.ds(pl.multiple_of(i * STEP, STEP), STEP)
            spec[grp, at] = to_spectrum(load(direct, grp, i, NT), into, spread)
            return 0

        lax.fori_loop(0, ST // STEP, spectrum_of, 0, unroll=True)
        if grp == 0:
            pl.semaphore_wait(barrier, len(peers))

        for it in range(ITERS):
            pack_spec(grp)
            sent = []
            stage = {}
            for n in (4, 5, 2, 3, 1, 0):
                for o in (2, 1, 3, 0):
                    if n or o:
                        c = go(
                            ("g", n, o), piece.at[grp, freqs[o]], land_g.at[grp, n, f],
                            at_src(*near[n], o),
                        )
                        stage.setdefault(n, []).append(c)
                        sent.append(c)
            land_g[grp, 0, f] = piece[grp, f]
            late = []

            def arrive(n):
                for c in stage[n]:
                    c.wait_recv()
                dl, dz = near[n]
                at = rows_at(dl, -dz)
                blocks = take_bins([land_g[grp, n, q] for q in range(NX)])
                for j in range(BL):
                    xs[grp, j, at] = blocks[j]
                return at

            def forward_to(name, at, dl, dz):
                c = go(name, xs.at[grp, :, at], xs.at[grp, :, at], at_src(dl, dz))
                late.append(c)
                sent.append(c)

            yield
            for n in (2, 3):
                at = arrive(n)
                forward_to(("gy", n), at, 1, 0)
            yield
            for n, w, way in ((4, 0, 1), (5, 1, -1)):
                at = arrive(n)
                half = rows_at(0, -2 * way, w)
                forward_to(("gd", n), at, 1, way)
                forward_to(("g3", n), at, 0, way)
                forward_to(("ge", n), half, 1, 2 * way)
                forward_to(("g4", n), half, 0, 2 * way)
                forward_to(("gy", n), at, 1, 0)
            arrive(0)
            arrive(1)
            yield
            for c in late:
                c.wait_recv()
            for c in sent:
                c.wait_send()

            def forward(j, _):
                x_high, x_low = halves(unfold(xs[grp, j]))
                both = mm(r_high[j], jnp.concatenate([x_high, x_low], axis=1))
                g = fold(both[:, :LN] + both[:, LN:] + mm(r_low[j], x_high))
                n = SRC // SH
                real = is_real((n, LN))
                turned = swap_parts(g[n:], real)
                y[grp, j] = g[:n] + jnp.where(real, -turned, turned)
                return 0

            lax.fori_loop(0, BL, forward, 0, unroll=True)

            pair = [
                go(("ra", dh), y.at[grp, :, rcv_rows(dh, 1)], r4a.at[grp, dh], at_rcv(0, 1))
                for dh in (1, 0)
            ]
            yield
            sent = list(pair)
            stage = []
            for dh, c in zip((1, 0), pair):
                c.wait_recv()
                total = y[grp, :, rcv_rows(dh, 0)] + r4a[grp, dh]
                pack_bins(grp, dh, [total[j] for j in range(BL)])
                for o in (2, 1, 3, 0):
                    if dh or o:
                        stage.append(
                            go(
                                ("rx", dh, o), piece_sum.at[grp, dh, freqs[o]],
                                land_r.at[grp, dh, f], at_rcv(dh, 0, o),
                            )
                        )
            land_r[grp, 0, f] = piece_sum[grp, 0, f]
            yield
            for c in stage:
                c.wait_recv()
            for c in sent + stage:
                c.wait_send()
            take_spec(grp, [land_r[grp, 0, q] + land_r[grp, 1, q] for q in range(NX)])

            def up(i, _):
                at = pl.ds(pl.multiple_of(i * STEP, STEP), STEP)
                x = jnp.where(keep(1, grp, i), to_time(spec[grp, at], collect, back), 0.0)
                store(out_minus, grp, i, x)
                spec[grp, at] = to_spectrum(x, into, spread)
                return 0

            lax.fori_loop(0, ST // STEP, up, 0, unroll=True)

            pack_spec(grp)
            stage = [[], []]
            for dh in (1, 0):
                for o in (2, 1, 3, 0):
                    if dh or o:
                        stage[dh].append(
                            go(
                                ("cx", dh, o), piece.at[grp, freqs[o]], land_f.at[grp, dh, f],
                                at_rcv(dh, 0, o),
                            )
                        )
            land_f[grp, 0, f] = piece[grp, f]
            yield
            pair = []
            for dh in (0, 1):
                for c in stage[dh]:
                    c.wait_recv()
                at = rcv_rows(dh, 0)
                blocks = take_bins([land_f[grp, dh, q] for q in range(NX)])
                for j in range(BL):
                    cs[grp, j, at] = blocks[j]
                pair.append(go(("cc", dh), cs.at[grp, :, at], cs.at[grp, :, at], at_rcv(0, 1)))
            yield
            for c in pair:
                c.wait_recv()
            for c in pair + stage[0] + stage[1]:
                c.wait_send()

            def adjoint(j, _):
                block = cs[grp, j]
                real = is_real(block.shape)
                turned = swap_parts(block, real)
                both = jnp.concatenate([block, jnp.where(real, turned, -turned)], axis=0)
                c_high, c_low = halves(unfold(both))
                both = mm(t_high[j], jnp.concatenate([c_high, c_low], axis=1))
                h[grp, j] = fold(both[:, :LN] + both[:, LN:] + mm(t_low[j], c_high))
                return 0

            lax.fori_loop(0, BL, adjoint, 0, unroll=True)

            sent = []
            stage = {}

            def part_to(name, slot, dl, dist, dest, part=None):
                target = rs.at[grp, slot]
                if part is not None:
                    target = rs.at[grp, slot, :, pl.ds(part * (ST // 2), ST // 2)]
                c = go(name, h.at[grp, :, rows_at(dl, dist, part)], target, at_src(*dest))
                stage[slot] = stage.get(slot, []) + [c]
                sent.append(c)

            for w, way in ((0, 1), (1, -1)):
                part_to(("se", w), 8 + w, 1, 4, (1, 2 * way), w)
                part_to(("s4", w), 6 + w, 0, 4, (0, 2 * way), w)
                part_to(("sd", w), 4 + w, 1, 3 * way, (1, way))
                part_to(("s3", w), 2 + w, 0, 3 * way, (0, way))
            for w, way in ((0, 1), (1, -1)):
                part_to(("sy", 2, w), 10 + w, 1, 2 * way, (1, 0))
            for w, way in ((0, 1), (1, -1)):
                part_to(("sy", 1, w), w, 1, way, (1, 0))

            last = {}

            def finish(n, blocks):
                pack_bins(grp, n, blocks)
                for o in (2, 1, 3, 0):
                    if n or o:
                        c = go(
                            ("sx", n, o), piece_sum.at[grp, n, freqs[o]], land_s.at[grp, n, f],
                            at_src(*near[n], o),
                        )
                        last.setdefault(n, []).append(c)
                        sent.append(c)

            def bins_of(total):
                return [total[j] for j in range(BL)]

            finish(1, [h[grp, j, rows_at(1, 0)] for j in range(BL)])
            finish(0, [h[grp, j, rows_at(0, 0)] for j in range(BL)])
            land_s[grp, 0, f] = piece_sum[grp, 0, f]
            yield
            for w, way in ((0, 1), (1, -1)):
                for c in stage[w]:
                    c.wait_recv()
                finish(2 + w, bins_of(h[grp, :, rows_at(0, way)] + rs[grp, w]))
            yield
            for w, way in ((0, 1), (1, -1)):
                for slot in (2 + w, 4 + w, 6 + w, 8 + w, 10 + w):
                    for c in stage[slot]:
                        c.wait_recv()
                total = h[grp, :, rows_at(0, 2 * way)] + rs[grp, 2 + w] + rs[grp, 4 + w]
                total = total + rs[grp, 10 + w]
                half = slice(w * (ST // 2), (w + 1) * (ST // 2))
                four = rs[grp, 6 + w, :, half] + rs[grp, 8 + w, :, half]
                some = [total[:, :8], total[:, 8:]] if ST == 16 else [total[:, :16], total[:, 16:]]
                some[w] = some[w] + four
                finish(4 + w, bins_of(jnp.concatenate(some, axis=1)))
            yield
            for n in range(6):
                for c in last[n]:
                    c.wait_recv()
            for c in sent:
                c.wait_send()
            pieces = []
            for q in range(NX):
                total = land_s[grp, 0, q]
                for n in range(1, 6):
                    total = total + land_s[grp, n, q]
                pieces.append(total)
            take_spec(grp, pieces)

            def down(i, _):
                at = pl.ds(pl.multiple_of(i * STEP, STEP), STEP)
                x = jnp.where(keep(0, grp, i), to_time(spec[grp, at], collect, back), 0.0)
                x = load(direct, grp, i, NT) + x
                if it < ITERS - 1:
                    spec[grp, at] = to_spectrum(x, into, spread)
                else:
                    store(out_plus, grp, i, x)
                return 0

            lax.fori_loop(0, ST // STEP, down, 0, unroll=True)

    running = [program(grp) for grp in range(GROUPS)]
    while running:
        for p in list(running):
            if next(p, 0) == 0:
                running.remove(p)


MESSAGES = 88 * GROUPS


def per_device(direct, reflection, onset_plus, onset_minus):
    vmem = pl.BlockSpec(memory_space=pltpu.VMEM)
    f32, bf16 = jnp.float32, jnp.bfloat16
    traces = jax.ShapeDtypeStruct((ST * SH, FP, NT), f32)
    return pl.pallas_call(
        kernel,
        out_shape=(traces, traces),
        in_specs=[vmem] * 8,
        out_specs=(vmem, vmem),
        scratch_shapes=[
            pltpu.VMEM((BL, 2 * SRC, RCV), bf16),
            pltpu.VMEM((BL, 2 * SRC, RCV), bf16),
            pltpu.VMEM((BL, RCV, 2 * SRC), bf16),
            pltpu.VMEM((BL, RCV, 2 * SRC), bf16),
            pltpu.VMEM((2, ST * SH, FP, LN), f32),
            pltpu.VMEM((GROUPS, ST, WIDE), f32),
            pltpu.VMEM((GROUPS, NX, PR, LN), f32),
            pltpu.VMEM((GROUPS, 6, NX, PR, LN), f32),
            pltpu.VMEM((GROUPS, 6, NX, PR, LN), f32),
            pltpu.VMEM((GROUPS, 2, NX, PR, LN), f32),
            pltpu.VMEM((GROUPS, 2, NX, PR, LN), f32),
            pltpu.VMEM((GROUPS, 6, NX, PR, LN), f32),
            pltpu.VMEM((GROUPS, BL, NS * ST, LN), f32),
            pltpu.VMEM((GROUPS, BL, NR * ST, LN), f32),
            pltpu.VMEM((GROUPS, 2, BL, ST, LN), f32),
            pltpu.VMEM((GROUPS, BL, NR * ST, LN), f32),
            pltpu.VMEM((GROUPS, BL, NS * ST, LN), f32),
            pltpu.VMEM((GROUPS, 12, BL, ST, LN), f32),
            pltpu.SemaphoreType.DMA((MESSAGES,)),
            pltpu.SemaphoreType.DMA((MESSAGES,)),
        ],
        compiler_params=pltpu.CompilerParams(
            collective_id=0, has_side_effects=True, vmem_limit_bytes=56 * 1024 * 1024
        ),
    )(direct, reflection, onset_plus.T, onset_minus.T, *[jnp.asarray(a) for a in tables()])


def solution(mesh):
    in_specs = (
        P(("rcv", "src"), "freq", None),
        P(None, "freq", "src", "rcv"),
        P(("rcv", "src"), "freq"),
        P(("src", "rcv"), "freq"),
    )
    out_specs = (P(("rcv", "src"), "freq", None), P(("src", "rcv"), "freq", None))
    return jax.shard_map(
        per_device, mesh=mesh, in_specs=in_specs, out_specs=out_specs, check_vma=False
    )
```

```python
import math

import jax
import jax.numpy as jnp
import ml_dtypes
import numpy as np
from jax import lax
from jax.experimental import pallas as pl
from jax.experimental.pallas import tpu as pltpu
from jax.sharding import PartitionSpec as P

FIRST_BIN = 32
ITERS = 2
MESH = pl.DeviceIdType.MESH

NF = 20
NX = 4
BL = NF // NX
FP = 16
GROUPS = 2
SH = GROUPS
PG = FP // GROUPS
ST = 32 // SH
NT = 1024
NZ = 8
LN = 128
SRC = 128
RCV = 512
HALF = RCV // 2
NR = 4
NY = 2 * NR
PR = ST + 8
COLS = 2 * NF
WIDE = COLS * FP
STEP = 8
ROWS = STEP * FP


def tables():
    k = (np.arange(NT)[:, None] * (FIRST_BIN + np.arange(NF))[None, :]) % NT
    angle = 2.0 * math.pi * k / NT
    scale = math.sqrt(2.0 / NT)
    table = np.stack([scale * np.cos(angle), -scale * np.sin(angle)], axis=2)
    table = table.reshape(NT, COLS).astype(np.float32)
    high = table.astype(ml_dtypes.bfloat16).astype(np.float32)
    low = (table - high).astype(ml_dtypes.bfloat16).astype(np.float32)
    into = np.zeros((2, NT, LN), np.float32)
    into[0, :, :COLS] = high
    into[0, :, COLS : 2 * COLS] = low
    into[1, :, :COLS] = high
    back = np.zeros((LN, NT), np.float32)
    back[:COLS] = high.T
    back[COLS : 2 * COLS] = high.T
    back[2 * COLS : 3 * COLS] = low.T
    spread = np.zeros((LN, WIDE), np.float32)
    collect = np.zeros((2, WIDE, LN), np.float32)
    for b in range(NF):
        for c in range(2):
            for p in range(FP):
                f, j = b // BL, b % BL
                lane = (f * LN + j * 32 if j < 4 else 4 * LN + f * 32) + c * FP + p
                col = 2 * b + c
                spread[col, lane] = 1
                spread[COLS + col, lane] = 1
                collect[0, lane, col] = 1
                collect[0, lane, 2 * COLS + col] = 1
                collect[1, lane, COLS + col] = 1
    return [a.astype(ml_dtypes.bfloat16) for a in (into, spread, collect, back)]


def halves(x):
    high = x.astype(jnp.bfloat16)
    return high, (x - high.astype(jnp.float32)).astype(jnp.bfloat16)


def mm(a, b):
    return lax.dot_general(a, b, (((1,), (0,)), ((), ())), preferred_element_type=jnp.float32)


def turn(x, lanes):
    lanes = lanes % LN
    return x if lanes == 0 else pltpu.roll(x, lanes, 1)


def pick(parts, i):
    group = lax.broadcasted_iota(jnp.int32, parts[0].shape, 1) // 32
    out = turn(parts[0], -i * 32)
    for k in range(1, len(parts)):
        out = jnp.where(group == k, turn(parts[k], (k - i) * 32), out)
    return out


def own_focus():
    row = lax.broadcasted_iota(jnp.int32, (ROWS, WIDE), 0) % FP
    lane = lax.broadcasted_iota(jnp.int32, (ROWS, WIDE), 1) % FP
    return row == lane


def to_spectrum(x, into, spread):
    high, low = halves(x)
    s = mm(high, into[0]) + mm(low, into[1])
    high, low = halves(s)
    e = mm(high, spread[...]) + mm(low, spread[...])
    e = jnp.where(own_focus(), e, 0.0).reshape(STEP, FP, WIDE)
    return jnp.sum(e, axis=1)


def to_time(z, collect, back):
    high = z.astype(jnp.bfloat16).astype(jnp.float32)
    low = z - high
    own = own_focus()

    def rows(v):
        v = jnp.broadcast_to(v[:, None, :], (STEP, FP, WIDE)).reshape(ROWS, WIDE)
        return jnp.where(own, v, 0.0).astype(jnp.bfloat16)

    g = mm(rows(high), collect[0]) + mm(rows(low), collect[1])
    return mm(g.astype(jnp.bfloat16), back[...])


def is_real(shape):
    return lax.broadcasted_iota(jnp.int32, shape, 1) % 32 < FP


def swap_parts(x, real):
    return jnp.where(real, turn(x, -FP), turn(x, FP))


def lane_block(shape):
    return lax.broadcasted_iota(jnp.int32, shape, 1) // PG % SH


def unfold(x):
    if SH == 1:
        return x
    at = lane_block(x.shape)
    return jnp.concatenate(
        [jnp.where(at == 0, x, turn(x, PG)), jnp.where(at == 1, x, turn(x, -PG))], axis=0
    )


def fold(x):
    if SH == 1:
        return x
    n = x.shape[0] // 2
    return jnp.where(lane_block((n, LN)) == 0, x[:n], x[n:])


def reorder(x, outer, inner):
    if SH == 1:
        return x
    return jnp.concatenate(
        [x[(o * SH + s) * inner : (o * SH + s + 1) * inner] for s in range(SH) for o in range(outer)],
        axis=0,
    )


def kernel(
    direct, refl, on_plus, on_minus, into, spread, collect, back,
    out_plus, out_minus,
    r_land, r_high, r_low, t_high, t_low, onset, spec, piece, piece_sum, land_g, land_r, land_f, land_s,
    xs, y, r4a, cs, h, rs, send_sem, recv_sem,
):
    f = lax.axis_index("freq")
    src = lax.axis_index("src")
    rcv = lax.axis_index("rcv")
    line = src // NZ
    z = src % NZ
    other = 1 - line
    high_y = rcv // 2
    core = rcv % 2
    freqs = [f] + [(f + o) % NX for o in range(1, NX)]

    def at_src(dl, dz, o=0):
        on = other if dl else line
        return (freqs[o], on * NZ + (z + dz + NZ) % NZ, rcv)

    def at_rcv(dl, dh, dc, o=0):
        hy = 1 - high_y if dh else high_y
        on = other if dl else line
        return (freqs[o], on * NZ + z, hy * 2 + (1 - core if dc else core))

    near = [0, 1, -1, 2, -2]
    column = [(0, 0), (1, 0), (0, 1), (1, 1)]
    peers = [at_src(0, k, o) for k in near for o in range(NX) if k or o]
    peers += [at_rcv(*k, 0, o) for k in column[1:] for o in range(NX)] + [at_rcv(0, 0, 1)]
    barrier = pltpu.get_barrier_semaphore()
    for peer in peers:
        pl.semaphore_signal(barrier, inc=1, device_id=peer, device_id_type=MESH)

    names = {}

    def copy(name, source, target, device):
        n = names.setdefault(name, len(names))
        return pltpu.make_async_remote_copy(
            src_ref=source, dst_ref=target, send_sem=send_sem.at[n], recv_sem=recv_sem.at[n],
            device_id=device, device_id_type=MESH,
        )

    def rows_at(dz, part=None):
        block = (z + dz + NZ) % NZ
        if part is None:
            return pl.ds(pl.multiple_of(block * ST, ST), ST)
        return pl.ds(pl.multiple_of(block * ST + part * (ST // 2), ST // 2), ST // 2)

    def rcv_rows(dl, dh, dc):
        block = (1 - high_y if dh else high_y) * 2 + (1 - core if dc else core)
        return pl.ds(pl.multiple_of((dl * NR + block) * ST, ST), ST)

    def lanes_of(on):
        return pl.ds(pl.multiple_of(on * HALF, HALF), HALF)

    swap = [
        copy(("r", j), refl.at[:, j, :, lanes_of(other)], r_land.at[j], at_rcv(1, 0, 0))
        for j in range(BL)
    ]

    def prepare(j):
        both = (refl[:, j, :, lanes_of(line)], r_land[j])
        block = jnp.concatenate(
            [
                b[c, (k * SH + s) * ST : (k * SH + s + 1) * ST]
                for s in range(SH)
                for c in range(2)
                for b in both
                for k in range(NR)
            ],
            axis=0,
        )
        block = reorder(block.T, NZ, ST)
        high, low = halves(block)
        t_high[j] = high
        t_low[j] = low
        high, low = halves(block.T)
        r_high[j] = high
        r_low[j] = low

    def prepare_onsets():
        whole = (ST * SH, FP, FP)
        eye = lax.broadcasted_iota(jnp.int32, whole, 1) == lax.broadcasted_iota(jnp.int32, whole, 2)
        for k, on in ((0, on_plus), (1, on_minus)):
            v = jnp.broadcast_to(on[...].astype(jnp.float32).T[:, None, :], whole)
            v = jnp.sum(jnp.where(eye, v, 0.0), axis=2, keepdims=True)
            onset[k] = jnp.broadcast_to(v, (ST * SH, FP, LN))

    def load(ref, grp, i, lanes):
        parts = [
            ref[pl.ds(pl.multiple_of(s * ST + i * STEP, STEP), STEP), grp * PG : (grp + 1) * PG]
            for s in range(SH)
        ]
        x = parts[0] if SH == 1 else jnp.concatenate(parts, axis=1)
        return x.reshape(ROWS, lanes)

    def store(ref, grp, i, x):
        x = x.reshape(STEP, FP, NT)
        for s in range(SH):
            at = pl.ds(pl.multiple_of(s * ST + i * STEP, STEP), STEP)
            ref[at, grp * PG : (grp + 1) * PG] = x[:, s * PG : (s + 1) * PG]

    def keep(k, grp, i):
        t = lax.broadcasted_iota(jnp.int32, (ROWS, NT), 1).astype(jnp.float32)
        return t < load(onset.at[k], grp, i, LN)[:, 0:1]

    parts_of = ST // 8

    def pack_spec(grp):
        last = spec[grp, :, 4 * LN :]
        parts = [last[8 * b : 8 * b + 8] for b in range(parts_of)]
        for q in range(NX):
            piece[grp, q, 0:ST] = spec[grp, :, q * LN : (q + 1) * LN]
            piece[grp, q, ST : ST + 8] = pick(parts, q)

    def pack_bins(grp, n, blocks):
        parts = [blocks[4][8 * b : 8 * b + 8] for b in range(parts_of)]
        for q in range(NX):
            piece_sum[grp, n, q, 0:ST] = pick(blocks[:4], q)
            piece_sum[grp, n, q, ST : ST + 8] = pick(parts, q)

    def take_spec(grp, pieces):
        for q in range(NX):
            spec[grp, :, q * LN : (q + 1) * LN] = pieces[q][0:ST]
        parts = [pieces[q][ST : ST + 8] for q in range(NX)]
        for b in range(parts_of):
            spec[grp, 8 * b : 8 * b + 8, 4 * LN :] = pick(parts, b)

    def take_bins(pieces):
        full = [p[0:ST] for p in pieces]
        parts = [p[ST : ST + 8] for p in pieces]
        out = [pick(full, j) for j in range(4)]
        out.append(jnp.concatenate([pick(parts, b) for b in range(parts_of)], axis=0))
        return out

    def program(grp):
        def go(name, source, target, device):
            c = copy((grp,) + name, source, target, device)
            c.start()
            return c

        def spectrum_of(i, _):
            at = pl.ds(pl.multiple_of(i * STEP, STEP), STEP)
            spec[grp, at] = to_spectrum(load(direct, grp, i, NT), into, spread)
            return 0

        lax.fori_loop(0, ST // STEP, spectrum_of, 0, unroll=True)
        if grp == 0:
            pl.semaphore_wait(barrier, len(peers))
            for c in swap:
                c.start()

        for it in range(ITERS):
            pack_spec(grp)
            sent = []
            stage = {}
            for n in (3, 4, 1, 2, 0):
                for o in (2, 1, 3, 0):
                    if n or o:
                        c = go(
                            ("g", n, o), piece.at[grp, freqs[o]], land_g.at[grp, n, f],
                            at_src(0, near[n], o),
                        )
                        stage.setdefault(n, []).append(c)
                        sent.append(c)
            land_g[grp, 0, f] = piece[grp, f]
            late = []

            def arrive(n):
                for c in stage[n]:
                    c.wait_recv()
                at = rows_at(-near[n])
                blocks = take_bins([land_g[grp, n, q] for q in range(NX)])
                for j in range(BL):
                    xs[grp, j, at] = blocks[j]
                return at

            def forward_to(name, at, dz):
                c = go(name, xs.at[grp, :, at], xs.at[grp, :, at], at_src(0, dz))
                late.append(c)
                sent.append(c)

            if it == 0 and grp == GROUPS - 1:
                prepare_onsets()
            yield
            for n, w, way in ((3, 0, 1), (4, 1, -1)):
                at = arrive(n)
                forward_to(("g3", n), at, way)
                forward_to(("g4", n), rows_at(-2 * way, w), 2 * way)
            for n in (1, 2, 0):
                arrive(n)
            yield
            for c in late:
                c.wait_recv()
            for c in sent:
                c.wait_send()

            def forward(j, _):
                x_high, x_low = halves(unfold(xs[grp, j]))
                both = mm(r_high[j], jnp.concatenate([x_high, x_low], axis=1))
                g = fold(both[:, :LN] + both[:, LN:] + mm(r_low[j], x_high))
                n = 2 * SRC // SH
                real = is_real((n, LN))
                turned = swap_parts(g[n:], real)
                y[grp, j] = g[:n] + jnp.where(real, -turned, turned)
                return 0

            for j in range(BL):
                if it == 0 and grp == 0:
                    swap[j].wait_recv()
                    prepare(j)
                forward(j, 0)

            order = (2, 3, 1, 0)
            pair = {
                n: go(
                    ("ra", n), y.at[grp, :, rcv_rows(*column[n], 1)], r4a.at[grp, n],
                    at_rcv(0, 0, 1),
                )
                for n in order
            }
            yield
            stage = []
            for n in order:
                pair[n].wait_recv()
                total = y[grp, :, rcv_rows(*column[n], 0)] + r4a[grp, n]
                pack_bins(grp, n, [total[j] for j in range(BL)])
                for o in (2, 1, 3, 0):
                    if n or o:
                        stage.append(
                            go(
                                ("rx", n, o), piece_sum.at[grp, n, freqs[o]],
                                land_r.at[grp, n, f], at_rcv(*column[n], 0, o),
                            )
                        )
            land_r[grp, 0, f] = piece_sum[grp, 0, f]
            yield
            for c in stage:
                c.wait_recv()
            for c in list(pair.values()) + stage:
                c.wait_send()
            take_spec(
                grp,
                [
                    (land_r[grp, 0, q] + land_r[grp, 1, q]) + (land_r[grp, 2, q] + land_r[grp, 3, q])
                    for q in range(NX)
                ],
            )

            def up(i, _):
                at = pl.ds(pl.multiple_of(i * STEP, STEP), STEP)
                x = jnp.where(keep(1, grp, i), to_time(spec[grp, at], collect, back), 0.0)
                store(out_minus, grp, i, x)
                spec[grp, at] = to_spectrum(x, into, spread)
                return 0

            lax.fori_loop(0, ST // STEP, up, 0, unroll=True)

            pack_spec(grp)
            stage = {}
            for n in order:
                for o in (2, 1, 3, 0):
                    if n or o:
                        c = go(
                            ("cx", n, o), piece.at[grp, freqs[o]], land_f.at[grp, n, f],
                            at_rcv(*column[n], 0, o),
                        )
                        stage.setdefault(n, []).append(c)
            land_f[grp, 0, f] = piece[grp, f]
            yield
            pair = []
            for n in (0, 1, 3, 2):
                for c in stage[n]:
                    c.wait_recv()
                at = rcv_rows(*column[n], 0)
                blocks = take_bins([land_f[grp, n, q] for q in range(NX)])
                for j in range(BL):
                    cs[grp, j, at] = blocks[j]
                pair.append(
                    go(("cc", n), cs.at[grp, :, at], cs.at[grp, :, at], at_rcv(0, 0, 1))
                )
            yield
            for c in pair:
                c.wait_recv()
            for c in pair + [c for n in order for c in stage[n]]:
                c.wait_send()

            def adjoint(j, _):
                block = cs[grp, j]
                real = is_real(block.shape)
                turned = swap_parts(block, real)
                both = jnp.concatenate([block, jnp.where(real, turned, -turned)], axis=0)
                c_high, c_low = halves(unfold(both))
                both = mm(t_high[j], jnp.concatenate([c_high, c_low], axis=1))
                h[grp, j] = fold(both[:, :LN] + both[:, LN:] + mm(t_low[j], c_high))
                return 0

            for j in range(BL):
                adjoint(j, 0)

            sent = []
            stage = [[], []]

            def part_to(name, w, slot, dist, dz, part=None):
                target = rs.at[grp, slot]
                if part is not None:
                    target = rs.at[grp, slot, :, pl.ds(part * (ST // 2), ST // 2)]
                c = go(name, h.at[grp, :, rows_at(dist, part)], target, at_src(0, dz))
                stage[w].append(c)
                sent.append(c)

            for w, way in ((0, 1), (1, -1)):
                part_to(("s4", w), w, 2 + w, 4, 2 * way, w)
                part_to(("s3", w), w, w, 3 * way, way)

            last = {}

            def finish(n, blocks):
                pack_bins(grp, n, blocks)
                for o in (2, 1, 3, 0):
                    if n or o:
                        c = go(
                            ("sx", n, o), piece_sum.at[grp, n, freqs[o]], land_s.at[grp, n, f],
                            at_src(0, near[n], o),
                        )
                        last.setdefault(n, []).append(c)
                        sent.append(c)

            def bins_of(total):
                return [total[j] for j in range(BL)]

            finish(1, [h[grp, j, rows_at(1)] for j in range(BL)])
            finish(2, [h[grp, j, rows_at(-1)] for j in range(BL)])
            finish(0, [h[grp, j, rows_at(0)] for j in range(BL)])
            land_s[grp, 0, f] = piece_sum[grp, 0, f]
            yield
            for w, way in ((0, 1), (1, -1)):
                for c in stage[w]:
                    c.wait_recv()
                total = h[grp, :, rows_at(2 * way)] + rs[grp, w]
                half = slice(w * (ST // 2), (w + 1) * (ST // 2))
                some = [total[:, : ST // 2], total[:, ST // 2 :]]
                some[w] = some[w] + rs[grp, 2 + w, :, half]
                finish(3 + w, bins_of(jnp.concatenate(some, axis=1)))
            yield
            for n in range(5):
                for c in last[n]:
                    c.wait_recv()
            for c in sent:
                c.wait_send()
            pieces = []
            for q in range(NX):
                total = land_s[grp, 0, q]
                for n in range(1, 5):
                    total = total + land_s[grp, n, q]
                pieces.append(total)
            take_spec(grp, pieces)

            def down(i, _):
                at = pl.ds(pl.multiple_of(i * STEP, STEP), STEP)
                x = jnp.where(keep(0, grp, i), to_time(spec[grp, at], collect, back), 0.0)
                x = load(direct, grp, i, NT) + x
                if it < ITERS - 1:
                    spec[grp, at] = to_spectrum(x, into, spread)
                else:
                    store(out_plus, grp, i, x)
                return 0

            lax.fori_loop(0, ST // STEP, down, 0, unroll=True)

    running = [program(grp) for grp in range(GROUPS)]
    while running:
        for p in list(running):
            if next(p, 0) == 0:
                running.remove(p)
    for c in swap:
        c.wait_send()


MESSAGES = 84 * GROUPS + BL


def per_device(direct, reflection, onset_plus, onset_minus):
    vmem = pl.BlockSpec(memory_space=pltpu.VMEM)
    f32, bf16 = jnp.float32, jnp.bfloat16
    traces = jax.ShapeDtypeStruct((ST * SH, FP, NT), f32)
    return pl.pallas_call(
        kernel,
        out_shape=(traces, traces),
        in_specs=[vmem] * 8,
        out_specs=(vmem, vmem),
        scratch_shapes=[
            pltpu.VMEM((BL, 2, SRC, HALF), f32),
            pltpu.VMEM((BL, 4 * SRC, HALF), bf16),
            pltpu.VMEM((BL, 4 * SRC, HALF), bf16),
            pltpu.VMEM((BL, HALF, 4 * SRC), bf16),
            pltpu.VMEM((BL, HALF, 4 * SRC), bf16),
            pltpu.VMEM((2, ST * SH, FP, LN), f32),
            pltpu.VMEM((GROUPS, ST, WIDE), f32),
            pltpu.VMEM((GROUPS, NX, PR, LN), f32),
            pltpu.VMEM((GROUPS, 5, NX, PR, LN), f32),
            pltpu.VMEM((GROUPS, 5, NX, PR, LN), f32),
            pltpu.VMEM((GROUPS, 4, NX, PR, LN), f32),
            pltpu.VMEM((GROUPS, 4, NX, PR, LN), f32),
            pltpu.VMEM((GROUPS, 5, NX, PR, LN), f32),
            pltpu.VMEM((GROUPS, BL, NZ * ST, LN), f32),
            pltpu.VMEM((GROUPS, BL, NY * ST, LN), f32),
            pltpu.VMEM((GROUPS, 4, BL, ST, LN), f32),
            pltpu.VMEM((GROUPS, BL, NY * ST, LN), f32),
            pltpu.VMEM((GROUPS, BL, NZ * ST, LN), f32),
            pltpu.VMEM((GROUPS, 4, BL, ST, LN), f32),
            pltpu.SemaphoreType.DMA((MESSAGES,)),
            pltpu.SemaphoreType.DMA((MESSAGES,)),
        ],
        compiler_params=pltpu.CompilerParams(
            collective_id=0, has_side_effects=True, vmem_limit_bytes=56 * 1024 * 1024
        ),
    )(direct, reflection, onset_plus.T, onset_minus.T, *[jnp.asarray(a) for a in tables()])


def solution(mesh):
    in_specs = (
        P(("rcv", "src"), "freq", None),
        P(None, "freq", "src", "rcv"),
        P(("rcv", "src"), "freq"),
        P(("src", "rcv"), "freq"),
    )
    out_specs = (P(("rcv", "src"), "freq", None), P(("src", "rcv"), "freq", None))
    return jax.shard_map(
        per_device, mesh=mesh, in_specs=in_specs, out_specs=out_specs, check_vma=False
    )
```

```python
import math

import jax
import jax.numpy as jnp
import ml_dtypes
import numpy as np
from jax import lax
from jax.experimental import pallas as pl
from jax.experimental.pallas import tpu as pltpu
from jax.sharding import PartitionSpec as P

FIRST_BIN = 32
ITERS = 2
MESH = pl.DeviceIdType.MESH

NF = 20
NX = 4
BL = NF // NX
FP = 16
GROUPS = 2
SH = GROUPS
PG = FP // GROUPS
ST = 32 // SH
NT = 1024
NZ = 8
LN = 128
SRC = 128
RCV = 512
HALF = RCV // 2
NR = 4
NY = 2 * NR
PR = ST + 8
COLS = 2 * NF
WIDE = COLS * FP
STEP = 8
ROWS = STEP * FP


def tables():
    k = (np.arange(NT)[:, None] * (FIRST_BIN + np.arange(NF))[None, :]) % NT
    angle = 2.0 * math.pi * k / NT
    scale = math.sqrt(2.0 / NT)
    table = np.stack([scale * np.cos(angle), -scale * np.sin(angle)], axis=2)
    table = table.reshape(NT, COLS).astype(np.float32)
    high = table.astype(ml_dtypes.bfloat16).astype(np.float32)
    low = (table - high).astype(ml_dtypes.bfloat16).astype(np.float32)
    into = np.zeros((2, NT, LN), np.float32)
    into[0, :, :COLS] = high
    into[0, :, COLS : 2 * COLS] = low
    into[1, :, :COLS] = high
    back = np.zeros((LN, NT), np.float32)
    back[:COLS] = high.T
    back[COLS : 2 * COLS] = high.T
    back[2 * COLS : 3 * COLS] = low.T
    spread = np.zeros((LN, WIDE), np.float32)
    collect = np.zeros((2, WIDE, LN), np.float32)
    for b in range(NF):
        for c in range(2):
            for p in range(FP):
                f, j = b // BL, b % BL
                lane = (f * LN + j * 32 if j < 4 else 4 * LN + f * 32) + c * FP + p
                col = 2 * b + c
                spread[col, lane] = 1
                spread[COLS + col, lane] = 1
                collect[0, lane, col] = 1
                collect[0, lane, 2 * COLS + col] = 1
                collect[1, lane, COLS + col] = 1
    return [a.astype(ml_dtypes.bfloat16) for a in (into, spread, collect, back)]


def halves(x):
    high = x.astype(jnp.bfloat16)
    return high, (x - high.astype(jnp.float32)).astype(jnp.bfloat16)


def mm(a, b):
    return lax.dot_general(a, b, (((1,), (0,)), ((), ())), preferred_element_type=jnp.float32)


def turn(x, lanes):
    lanes = lanes % LN
    return x if lanes == 0 else pltpu.roll(x, lanes, 1)


def pick(parts, i):
    group = lax.broadcasted_iota(jnp.int32, parts[0].shape, 1) // 32
    out = turn(parts[0], -i * 32)
    for k in range(1, len(parts)):
        out = jnp.where(group == k, turn(parts[k], (k - i) * 32), out)
    return out


def own_focus():
    row = lax.broadcasted_iota(jnp.int32, (ROWS, WIDE), 0) % FP
    lane = lax.broadcasted_iota(jnp.int32, (ROWS, WIDE), 1) % FP
    return row == lane


def to_spectrum(x, into, spread):
    high, low = halves(x)
    s = mm(high, into[0]) + mm(low, into[1])
    high, low = halves(s)
    e = mm(high, spread[...]) + mm(low, spread[...])
    e = jnp.where(own_focus(), e, 0.0).reshape(STEP, FP, WIDE)
    return jnp.sum(e, axis=1)


def to_time(z, collect, back):
    high = z.astype(jnp.bfloat16).astype(jnp.float32)
    low = z - high
    own = own_focus()

    def rows(v):
        v = jnp.broadcast_to(v[:, None, :], (STEP, FP, WIDE)).reshape(ROWS, WIDE)
        return jnp.where(own, v, 0.0).astype(jnp.bfloat16)

    g = mm(rows(high), collect[0]) + mm(rows(low), collect[1])
    return mm(g.astype(jnp.bfloat16), back[...])


def is_real(shape):
    return lax.broadcasted_iota(jnp.int32, shape, 1) % 32 < FP


def swap_parts(x, real):
    return jnp.where(real, turn(x, -FP), turn(x, FP))


def lane_block(shape):
    return lax.broadcasted_iota(jnp.int32, shape, 1) // PG % SH


def unfold(x):
    if SH == 1:
        return x
    at = lane_block(x.shape)
    return jnp.concatenate(
        [jnp.where(at == 0, x, turn(x, PG)), jnp.where(at == 1, x, turn(x, -PG))], axis=0
    )


def fold(x):
    if SH == 1:
        return x
    n = x.shape[0] // 2
    return jnp.where(lane_block((n, LN)) == 0, x[:n], x[n:])


def reorder(x, outer, inner):
    if SH == 1:
        return x
    return jnp.concatenate(
        [x[(o * SH + s) * inner : (o * SH + s + 1) * inner] for s in range(SH) for o in range(outer)],
        axis=0,
    )


def kernel(
    direct_in, refl_in, on_plus, on_minus, into_in, spread_in, collect_in, back_in,
    out_plus, out_minus, direct, refl, into, spread, collect, back, local_sem,
    r_land, r_high, r_low, t_high, t_low, onset, spec, piece, piece_sum, land_g, land_r, land_f, land_s,
    xs, y, r4a, cs, h, rs, send_sem, recv_sem,
):
    f = lax.axis_index("freq")
    src = lax.axis_index("src")
    rcv = lax.axis_index("rcv")
    line = src // NZ
    z = src % NZ
    other = 1 - line
    high_y = rcv // 2
    core = rcv % 2
    freqs = [f] + [(f + o) % NX for o in range(1, NX)]

    def at_src(dl, dz, o=0):
        on = other if dl else line
        return (freqs[o], on * NZ + (z + dz + NZ) % NZ, rcv)

    def at_rcv(dl, dh, dc, o=0):
        hy = 1 - high_y if dh else high_y
        on = other if dl else line
        return (freqs[o], on * NZ + z, hy * 2 + (1 - core if dc else core))

    near = [0, 1, -1, 2, -2]
    column = [(0, 0), (1, 0), (0, 1), (1, 1)]
    peers = [at_src(0, k, o) for k in near for o in range(NX) if k or o]
    peers += [at_rcv(*k, 0, o) for k in column[1:] for o in range(NX)] + [at_rcv(0, 0, 1)]
    barrier = pltpu.get_barrier_semaphore()
    for peer in peers:
        pl.semaphore_signal(barrier, inc=1, device_id=peer, device_id_type=MESH)

    def lanes_of(on):
        return pl.ds(pl.multiple_of(on * HALF, HALF), HALF)

    loads = [(into_in, into), (spread_in, spread), (direct_in, direct), (collect_in, collect)]
    loads += [(back_in, back), (refl_in.at[:, :, :, lanes_of(line)], refl)]
    loads = [
        pltpu.make_async_copy(a, b, local_sem.at[n]) for n, (a, b) in enumerate(loads)
    ]
    for c in loads:
        c.start()

    names = {}

    def copy(name, source, target, device):
        n = names.setdefault(name, len(names))
        return pltpu.make_async_remote_copy(
            src_ref=source, dst_ref=target, send_sem=send_sem.at[n], recv_sem=recv_sem.at[n],
            device_id=device, device_id_type=MESH,
        )

    def rows_at(dz, part=None):
        block = (z + dz + NZ) % NZ
        if part is None:
            return pl.ds(pl.multiple_of(block * ST, ST), ST)
        return pl.ds(pl.multiple_of(block * ST + part * (ST // 2), ST // 2), ST // 2)

    def rcv_rows(dl, dh, dc):
        block = (1 - high_y if dh else high_y) * 2 + (1 - core if dc else core)
        return pl.ds(pl.multiple_of((dl * NR + block) * ST, ST), ST)

    swap = [
        copy(("r", j), refl_in.at[:, j, :, lanes_of(other)], r_land.at[j], at_rcv(1, 0, 0))
        for j in range(BL)
    ]

    def prepare(j):
        both = (refl[:, j], r_land[j])
        block = jnp.concatenate(
            [
                b[c, (k * SH + s) * ST : (k * SH + s + 1) * ST]
                for s in range(SH)
                for c in range(2)
                for b in both
                for k in range(NR)
            ],
            axis=0,
        )
        block = reorder(block.T, NZ, ST)
        high, low = halves(block)
        t_high[j] = high
        t_low[j] = low
        high, low = halves(block.T)
        r_high[j] = high
        r_low[j] = low

    def prepare_onsets():
        whole = (ST * SH, FP, FP)
        eye = lax.broadcasted_iota(jnp.int32, whole, 1) == lax.broadcasted_iota(jnp.int32, whole, 2)
        for k, on in ((0, on_plus), (1, on_minus)):
            v = jnp.broadcast_to(on[...].astype(jnp.float32).T[:, None, :], whole)
            v = jnp.sum(jnp.where(eye, v, 0.0), axis=2, keepdims=True)
            onset[k] = jnp.broadcast_to(v, (ST * SH, FP, LN))

    def load(ref, grp, i, lanes):
        parts = [
            ref[pl.ds(pl.multiple_of(s * ST + i * STEP, STEP), STEP), grp * PG : (grp + 1) * PG]
            for s in range(SH)
        ]
        x = parts[0] if SH == 1 else jnp.concatenate(parts, axis=1)
        return x.reshape(ROWS, lanes)

    def store(ref, grp, i, x):
        x = x.reshape(STEP, FP, NT)
        for s in range(SH):
            at = pl.ds(pl.multiple_of(s * ST + i * STEP, STEP), STEP)
            ref[at, grp * PG : (grp + 1) * PG] = x[:, s * PG : (s + 1) * PG]

    def keep(k, grp, i):
        t = lax.broadcasted_iota(jnp.int32, (ROWS, NT), 1).astype(jnp.float32)
        return t < load(onset.at[k], grp, i, LN)[:, 0:1]

    parts_of = ST // 8

    def pack_spec(grp):
        last = spec[grp, :, 4 * LN :]
        parts = [last[8 * b : 8 * b + 8] for b in range(parts_of)]
        for q in range(NX):
            piece[grp, q, 0:ST] = spec[grp, :, q * LN : (q + 1) * LN]
            piece[grp, q, ST : ST + 8] = pick(parts, q)

    def pack_bins(grp, n, blocks):
        parts = [blocks[4][8 * b : 8 * b + 8] for b in range(parts_of)]
        for q in range(NX):
            piece_sum[grp, n, q, 0:ST] = pick(blocks[:4], q)
            piece_sum[grp, n, q, ST : ST + 8] = pick(parts, q)

    def take_spec(grp, pieces):
        for q in range(NX):
            spec[grp, :, q * LN : (q + 1) * LN] = pieces[q][0:ST]
        parts = [pieces[q][ST : ST + 8] for q in range(NX)]
        for b in range(parts_of):
            spec[grp, 8 * b : 8 * b + 8, 4 * LN :] = pick(parts, b)

    def take_bins(pieces):
        full = [p[0:ST] for p in pieces]
        parts = [p[ST : ST + 8] for p in pieces]
        out = [pick(full, j) for j in range(4)]
        out.append(jnp.concatenate([pick(parts, b) for b in range(parts_of)], axis=0))
        return out

    def program(grp):
        def go(name, source, target, device):
            c = copy((grp,) + name, source, target, device)
            c.start()
            return c

        def spectrum_of(i, _):
            at = pl.ds(pl.multiple_of(i * STEP, STEP), STEP)
            spec[grp, at] = to_spectrum(load(direct, grp, i, NT), into, spread)
            return 0

        if grp == 0:
            for c in loads[:3]:
                c.wait()
        lax.fori_loop(0, ST // STEP, spectrum_of, 0, unroll=True)
        if grp == 0:
            pl.semaphore_wait(barrier, len(peers))
            for c in swap:
                c.start()

        for it in range(ITERS):
            pack_spec(grp)
            sent = []
            stage = {}
            for n in (3, 4, 1, 2, 0):
                for o in (2, 1, 3, 0):
                    if n or o:
                        c = go(
                            ("g", n, o), piece.at[grp, freqs[o]], land_g.at[grp, n, f],
                            at_src(0, near[n], o),
                        )
                        stage.setdefault(n, []).append(c)
                        sent.append(c)
            land_g[grp, 0, f] = piece[grp, f]
            late = []

            def arrive(n):
                for c in stage[n]:
                    c.wait_recv()
                at = rows_at(-near[n])
                blocks = take_bins([land_g[grp, n, q] for q in range(NX)])
                for j in range(BL):
                    xs[grp, j, at] = blocks[j]
                return at

            def forward_to(name, at, dz):
                c = go(name, xs.at[grp, :, at], xs.at[grp, :, at], at_src(0, dz))
                late.append(c)
                sent.append(c)

            if it == 0 and grp == GROUPS - 1:
                prepare_onsets()
                for c in loads[3:]:
                    c.wait()
            yield
            for n, w, way in ((3, 0, 1), (4, 1, -1)):
                at = arrive(n)
                forward_to(("g3", n), at, way)
                forward_to(("g4", n), rows_at(-2 * way, w), 2 * way)
            for n in (1, 2, 0):
                arrive(n)
            yield
            for c in late:
                c.wait_recv()
            for c in sent:
                c.wait_send()

            def forward(j, _):
                x_high, x_low = halves(unfold(xs[grp, j]))
                both = mm(r_high[j], jnp.concatenate([x_high, x_low], axis=1))
                g = fold(both[:, :LN] + both[:, LN:] + mm(r_low[j], x_high))
                n = 2 * SRC // SH
                real = is_real((n, LN))
                turned = swap_parts(g[n:], real)
                y[grp, j] = g[:n] + jnp.where(real, -turned, turned)
                return 0

            for j in range(BL):
                if it == 0 and grp == 0:
                    swap[j].wait_recv()
                    prepare(j)
                forward(j, 0)

            order = (2, 3, 1, 0)
            pair = {
                n: go(
                    ("ra", n), y.at[grp, :, rcv_rows(*column[n], 1)], r4a.at[grp, n],
                    at_rcv(0, 0, 1),
                )
                for n in order
            }
            yield
            stage = []
            for n in order:
                pair[n].wait_recv()
                total = y[grp, :, rcv_rows(*column[n], 0)] + r4a[grp, n]
                pack_bins(grp, n, [total[j] for j in range(BL)])
                for o in (2, 1, 3, 0):
                    if n or o:
                        stage.append(
                            go(
                                ("rx", n, o), piece_sum.at[grp, n, freqs[o]],
                                land_r.at[grp, n, f], at_rcv(*column[n], 0, o),
                            )
                        )
            land_r[grp, 0, f] = piece_sum[grp, 0, f]
            yield
            for c in stage:
                c.wait_recv()
            for c in list(pair.values()) + stage:
                c.wait_send()
            take_spec(
                grp,
                [
                    (land_r[grp, 0, q] + land_r[grp, 1, q]) + (land_r[grp, 2, q] + land_r[grp, 3, q])
                    for q in range(NX)
                ],
            )

            def up(i, _):
                at = pl.ds(pl.multiple_of(i * STEP, STEP), STEP)
                x = jnp.where(keep(1, grp, i), to_time(spec[grp, at], collect, back), 0.0)
                store(out_minus, grp, i, x)
                spec[grp, at] = to_spectrum(x, into, spread)
                return 0

            lax.fori_loop(0, ST // STEP, up, 0, unroll=True)

            pack_spec(grp)
            stage = {}
            for n in order:
                for o in (2, 1, 3, 0):
                    if n or o:
                        c = go(
                            ("cx", n, o), piece.at[grp, freqs[o]], land_f.at[grp, n, f],
                            at_rcv(*column[n], 0, o),
                        )
                        stage.setdefault(n, []).append(c)
            land_f[grp, 0, f] = piece[grp, f]
            yield
            pair = []
            for n in (0, 1, 3, 2):
                for c in stage[n]:
                    c.wait_recv()
                at = rcv_rows(*column[n], 0)
                blocks = take_bins([land_f[grp, n, q] for q in range(NX)])
                for j in range(BL):
                    cs[grp, j, at] = blocks[j]
                pair.append(
                    go(("cc", n), cs.at[grp, :, at], cs.at[grp, :, at], at_rcv(0, 0, 1))
                )
            yield
            for c in pair:
                c.wait_recv()
            for c in pair + [c for n in order for c in stage[n]]:
                c.wait_send()

            def adjoint(j, _):
                block = cs[grp, j]
                real = is_real(block.shape)
                turned = swap_parts(block, real)
                both = jnp.concatenate([block, jnp.where(real, turned, -turned)], axis=0)
                c_high, c_low = halves(unfold(both))
                both = mm(t_high[j], jnp.concatenate([c_high, c_low], axis=1))
                h[grp, j] = fold(both[:, :LN] + both[:, LN:] + mm(t_low[j], c_high))
                return 0

            for j in range(BL):
                adjoint(j, 0)

            sent = []
            stage = [[], []]

            def part_to(name, w, slot, dist, dz, part=None):
                target = rs.at[grp, slot]
                if part is not None:
                    target = rs.at[grp, slot, :, pl.ds(part * (ST // 2), ST // 2)]
                c = go(name, h.at[grp, :, rows_at(dist, part)], target, at_src(0, dz))
                stage[w].append(c)
                sent.append(c)

            for w, way in ((0, 1), (1, -1)):
                part_to(("s4", w), w, 2 + w, 4, 2 * way, w)
                part_to(("s3", w), w, w, 3 * way, way)

            last = {}

            def finish(n, blocks):
                pack_bins(grp, n, blocks)
                for o in (2, 1, 3, 0):
                    if n or o:
                        c = go(
                            ("sx", n, o), piece_sum.at[grp, n, freqs[o]], land_s.at[grp, n, f],
                            at_src(0, near[n], o),
                        )
                        last.setdefault(n, []).append(c)
                        sent.append(c)

            def bins_of(total):
                return [total[j] for j in range(BL)]

            finish(1, [h[grp, j, rows_at(1)] for j in range(BL)])
            finish(2, [h[grp, j, rows_at(-1)] for j in range(BL)])
            finish(0, [h[grp, j, rows_at(0)] for j in range(BL)])
            land_s[grp, 0, f] = piece_sum[grp, 0, f]
            yield
            for w, way in ((0, 1), (1, -1)):
                for c in stage[w]:
                    c.wait_recv()
                total = h[grp, :, rows_at(2 * way)] + rs[grp, w]
                half = slice(w * (ST // 2), (w + 1) * (ST // 2))
                some = [total[:, : ST // 2], total[:, ST // 2 :]]
                some[w] = some[w] + rs[grp, 2 + w, :, half]
                finish(3 + w, bins_of(jnp.concatenate(some, axis=1)))
            yield
            for n in range(5):
                for c in last[n]:
                    c.wait_recv()
            for c in sent:
                c.wait_send()
            pieces = []
            for q in range(NX):
                total = land_s[grp, 0, q]
                for n in range(1, 5):
                    total = total + land_s[grp, n, q]
                pieces.append(total)
            take_spec(grp, pieces)

            def down(i, _):
                at = pl.ds(pl.multiple_of(i * STEP, STEP), STEP)
                x = jnp.where(keep(0, grp, i), to_time(spec[grp, at], collect, back), 0.0)
                x = load(direct, grp, i, NT) + x
                if it < ITERS - 1:
                    spec[grp, at] = to_spectrum(x, into, spread)
                else:
                    store(out_plus, grp, i, x)
                return 0

            lax.fori_loop(0, ST // STEP, down, 0, unroll=True)

    running = [program(grp) for grp in range(GROUPS)]
    while running:
        for p in list(running):
            if next(p, 0) == 0:
                running.remove(p)
    for c in swap:
        c.wait_send()


MESSAGES = 84 * GROUPS + BL


def per_device(direct, reflection, onset_plus, onset_minus):
    vmem = pl.BlockSpec(memory_space=pltpu.VMEM)
    hbm = pl.BlockSpec(memory_space=pl.ANY)
    f32, bf16 = jnp.float32, jnp.bfloat16
    traces = pltpu.VMEM((ST * SH, FP, NT), f32)
    return pl.pallas_call(
        kernel,
        out_shape=(traces, traces),
        in_specs=[hbm, hbm, vmem, vmem, hbm, hbm, hbm, hbm],
        out_specs=(vmem, vmem),
        scratch_shapes=[
            pltpu.VMEM((ST * SH, FP, NT), f32),
            pltpu.VMEM((2, BL, SRC, HALF), f32),
            pltpu.VMEM((2, NT, LN), bf16),
            pltpu.VMEM((LN, WIDE), bf16),
            pltpu.VMEM((2, WIDE, LN), bf16),
            pltpu.VMEM((LN, NT), bf16),
            pltpu.SemaphoreType.DMA((6 + 2 * GROUPS,)),
            pltpu.VMEM((BL, 2, SRC, HALF), f32),
            pltpu.VMEM((BL, 4 * SRC, HALF), bf16),
            pltpu.VMEM((BL, 4 * SRC, HALF), bf16),
            pltpu.VMEM((BL, HALF, 4 * SRC), bf16),
            pltpu.VMEM((BL, HALF, 4 * SRC), bf16),
            pltpu.VMEM((2, ST * SH, FP, LN), f32),
            pltpu.VMEM((GROUPS, ST, WIDE), f32),
            pltpu.VMEM((GROUPS, NX, PR, LN), f32),
            pltpu.VMEM((GROUPS, 5, NX, PR, LN), f32),
            pltpu.VMEM((GROUPS, 5, NX, PR, LN), f32),
            pltpu.VMEM((GROUPS, 4, NX, PR, LN), f32),
            pltpu.VMEM((GROUPS, 4, NX, PR, LN), f32),
            pltpu.VMEM((GROUPS, 5, NX, PR, LN), f32),
            pltpu.VMEM((GROUPS, BL, NZ * ST, LN), f32),
            pltpu.VMEM((GROUPS, BL, NY * ST, LN), f32),
            pltpu.VMEM((GROUPS, 4, BL, ST, LN), f32),
            pltpu.VMEM((GROUPS, BL, NY * ST, LN), f32),
            pltpu.VMEM((GROUPS, BL, NZ * ST, LN), f32),
            pltpu.VMEM((GROUPS, 4, BL, ST, LN), f32),
            pltpu.SemaphoreType.DMA((MESSAGES,)),
            pltpu.SemaphoreType.DMA((MESSAGES,)),
        ],
        compiler_params=pltpu.CompilerParams(
            collective_id=0, has_side_effects=True, vmem_limit_bytes=58 * 1024 * 1024
        ),
    )(direct, reflection, onset_plus.T, onset_minus.T, *[jnp.asarray(a) for a in tables()])


def solution(mesh):
    in_specs = (
        P(("rcv", "src"), "freq", None),
        P(None, "freq", "src", "rcv"),
        P(("rcv", "src"), "freq"),
        P(("src", "rcv"), "freq"),
    )
    out_specs = (P(("rcv", "src"), "freq", None), P(("src", "rcv"), "freq", None))
    return jax.shard_map(
        per_device, mesh=mesh, in_specs=in_specs, out_specs=out_specs, check_vma=False
    )
```

```python
import math

import jax
import jax.numpy as jnp
import ml_dtypes
import numpy as np
from jax import lax
from jax.experimental import pallas as pl
from jax.experimental.pallas import tpu as pltpu
from jax.sharding import PartitionSpec as P

FIRST_BIN = 32
ITERS = 2
MESH = pl.DeviceIdType.MESH

NF = 20
NX = 4
BL = NF // NX
FP = 16
GROUPS = 2
SH = GROUPS
PG = FP // GROUPS
ST = 32 // SH
NT = 1024
NZ = 8
LN = 128
SRC = 128
RCV = 512
HALF = RCV // 2
NR = 4
NY = 2 * NR
PR = ST + 8
COLS = 2 * NF
WIDE = COLS * FP
STEP = 8
ROWS = STEP * FP


def tables():
    k = (np.arange(NT)[:, None] * (FIRST_BIN + np.arange(NF))[None, :]) % NT
    angle = 2.0 * math.pi * k / NT
    scale = math.sqrt(2.0 / NT)
    table = np.stack([scale * np.cos(angle), -scale * np.sin(angle)], axis=2)
    table = table.reshape(NT, COLS).astype(np.float32)
    high = table.astype(ml_dtypes.bfloat16).astype(np.float32)
    low = (table - high).astype(ml_dtypes.bfloat16).astype(np.float32)
    into = np.zeros((2, NT, LN), np.float32)
    into[0, :, :COLS] = high
    into[0, :, COLS : 2 * COLS] = low
    into[1, :, :COLS] = high
    back = np.zeros((LN, NT), np.float32)
    back[:COLS] = high.T
    back[COLS : 2 * COLS] = high.T
    back[2 * COLS : 3 * COLS] = low.T
    spread = np.zeros((LN, WIDE), np.float32)
    collect = np.zeros((2, WIDE, LN), np.float32)
    for b in range(NF):
        for c in range(2):
            for p in range(FP):
                f, j = b // BL, b % BL
                lane = (f * LN + j * 32 if j < 4 else 4 * LN + f * 32) + c * FP + p
                col = 2 * b + c
                spread[col, lane] = 1
                spread[COLS + col, lane] = 1
                collect[0, lane, col] = 1
                collect[0, lane, 2 * COLS + col] = 1
                collect[1, lane, COLS + col] = 1
    return [a.astype(ml_dtypes.bfloat16) for a in (into, spread, collect, back)]


def halves(x):
    high = x.astype(jnp.bfloat16)
    return high, (x - high.astype(jnp.float32)).astype(jnp.bfloat16)


def mm(a, b):
    return lax.dot_general(a, b, (((1,), (0,)), ((), ())), preferred_element_type=jnp.float32)


def turn(x, lanes):
    lanes = lanes % LN
    return x if lanes == 0 else pltpu.roll(x, lanes, 1)


def pick(parts, i):
    group = lax.broadcasted_iota(jnp.int32, parts[0].shape, 1) // 32
    out = turn(parts[0], -i * 32)
    for k in range(1, len(parts)):
        out = jnp.where(group == k, turn(parts[k], (k - i) * 32), out)
    return out


def own_focus():
    row = lax.broadcasted_iota(jnp.int32, (ROWS, WIDE), 0) % FP
    lane = lax.broadcasted_iota(jnp.int32, (ROWS, WIDE), 1) % FP
    return row == lane


def to_spectrum(x, into, spread):
    high, low = halves(x)
    s = mm(high, into[0]) + mm(low, into[1])
    high, low = halves(s)
    e = mm(high, spread[...]) + mm(low, spread[...])
    e = jnp.where(own_focus(), e, 0.0).reshape(STEP, FP, WIDE)
    return jnp.sum(e, axis=1)


def to_time(z, collect, back):
    high = z.astype(jnp.bfloat16).astype(jnp.float32)
    low = z - high
    own = own_focus()

    def rows(v):
        v = jnp.broadcast_to(v[:, None, :], (STEP, FP, WIDE)).reshape(ROWS, WIDE)
        return jnp.where(own, v, 0.0).astype(jnp.bfloat16)

    g = mm(rows(high), collect[0]) + mm(rows(low), collect[1])
    return mm(g.astype(jnp.bfloat16), back[...])


def is_real(shape):
    return lax.broadcasted_iota(jnp.int32, shape, 1) % 32 < FP


def swap_parts(x, real):
    return jnp.where(real, turn(x, -FP), turn(x, FP))


def lane_block(shape):
    return lax.broadcasted_iota(jnp.int32, shape, 1) // PG % SH


def unfold(x):
    if SH == 1:
        return x
    at = lane_block(x.shape)
    return jnp.concatenate(
        [jnp.where(at == 0, x, turn(x, PG)), jnp.where(at == 1, x, turn(x, -PG))], axis=0
    )


def fold(x):
    if SH == 1:
        return x
    n = x.shape[0] // 2
    return jnp.where(lane_block((n, LN)) == 0, x[:n], x[n:])


def reorder(x, outer, inner):
    if SH == 1:
        return x
    return jnp.concatenate(
        [x[(o * SH + s) * inner : (o * SH + s + 1) * inner] for s in range(SH) for o in range(outer)],
        axis=0,
    )


def kernel(
    direct_in, refl_in, on_plus, on_minus, into_in, spread_in, collect_in, back_in,
    out_plus, out_minus, direct, refl, into, spread, collect, back, local_sem,
    r_land, r_high, r_low, t_high, t_low, onset, spec, piece, piece_sum, land_g, land_r, land_f, land_s,
    xs, y, r4a, cs, h, rs, send_sem, recv_sem,
):
    f = lax.axis_index("freq")
    src = lax.axis_index("src")
    rcv = lax.axis_index("rcv")
    line = src // NZ
    z = src % NZ
    other = 1 - line
    high_y = rcv // 2
    core = rcv % 2
    freqs = [f] + [(f + o) % NX for o in range(1, NX)]

    def at_src(dl, dz, o=0):
        on = other if dl else line
        return (freqs[o], on * NZ + (z + dz + NZ) % NZ, rcv)

    def at_rcv(dl, dh, dc, o=0):
        hy = 1 - high_y if dh else high_y
        on = other if dl else line
        return (freqs[o], on * NZ + z, hy * 2 + (1 - core if dc else core))

    near = [0, 1, -1, 2, -2]
    column = [(0, 0), (1, 0), (0, 1), (1, 1)]
    peers = [at_src(0, k, o) for k in near for o in range(NX) if k or o]
    peers += [at_rcv(*k, 0, o) for k in column[1:] for o in range(NX)] + [at_rcv(0, 0, 1)]
    barrier = pltpu.get_barrier_semaphore()
    for peer in peers:
        pl.semaphore_signal(barrier, inc=1, device_id=peer, device_id_type=MESH)

    def lanes_of(on):
        return pl.ds(pl.multiple_of(on * HALF, HALF), HALF)

    loads = [(into_in, into), (spread_in, spread), (direct_in, direct), (collect_in, collect)]
    loads += [(back_in, back), (refl_in.at[:, :, :, lanes_of(line)], refl)]
    loads = [
        pltpu.make_async_copy(a, b, local_sem.at[n]) for n, (a, b) in enumerate(loads)
    ]
    for c in loads:
        c.start()

    names = {}

    def copy(name, source, target, device):
        n = names.setdefault(name, len(names))
        return pltpu.make_async_remote_copy(
            src_ref=source, dst_ref=target, send_sem=send_sem.at[n], recv_sem=recv_sem.at[n],
            device_id=device, device_id_type=MESH,
        )

    def rows_at(dz, part=None):
        block = (z + dz + NZ) % NZ
        if part is None:
            return pl.ds(pl.multiple_of(block * ST, ST), ST)
        return pl.ds(pl.multiple_of(block * ST + part * (ST // 2), ST // 2), ST // 2)

    def rcv_rows(dl, dh, dc):
        block = (1 - high_y if dh else high_y) * 2 + (1 - core if dc else core)
        return pl.ds(pl.multiple_of((dl * NR + block) * ST, ST), ST)

    swap = [
        copy(("r", j), refl_in.at[:, j, :, lanes_of(other)], r_land.at[j], at_rcv(1, 0, 0))
        for j in range(BL)
    ]

    def prepare(j):
        both = (refl[:, j], r_land[j])
        block = jnp.concatenate(
            [
                b[c, (k * SH + s) * ST : (k * SH + s + 1) * ST]
                for s in range(SH)
                for c in range(2)
                for b in both
                for k in range(NR)
            ],
            axis=0,
        )
        block = reorder(block.T, NZ, ST)
        high, low = halves(block)
        t_high[j] = high
        t_low[j] = low
        high, low = halves(block.T)
        r_high[j] = high
        r_low[j] = low

    def prepare_onsets():
        whole = (ST * SH, FP, FP)
        eye = lax.broadcasted_iota(jnp.int32, whole, 1) == lax.broadcasted_iota(jnp.int32, whole, 2)
        for k, on in ((0, on_plus), (1, on_minus)):
            v = jnp.broadcast_to(on[...].astype(jnp.float32).T[:, None, :], whole)
            v = jnp.sum(jnp.where(eye, v, 0.0), axis=2, keepdims=True)
            onset[k] = jnp.broadcast_to(v, (ST * SH, FP, LN))

    def load(ref, grp, i, lanes):
        parts = [
            ref[pl.ds(pl.multiple_of(s * ST + i * STEP, STEP), STEP), grp * PG : (grp + 1) * PG]
            for s in range(SH)
        ]
        x = parts[0] if SH == 1 else jnp.concatenate(parts, axis=1)
        return x.reshape(ROWS, lanes)

    def store(ref, grp, i, x):
        x = x.reshape(STEP, FP, NT)
        for s in range(SH):
            at = pl.ds(pl.multiple_of(s * ST + i * STEP, STEP), STEP)
            ref[at, grp * PG : (grp + 1) * PG] = x[:, s * PG : (s + 1) * PG]

    def keep(k, grp, i):
        t = lax.broadcasted_iota(jnp.int32, (ROWS, NT), 1).astype(jnp.float32)
        return t < load(onset.at[k], grp, i, LN)[:, 0:1]

    parts_of = ST // 8

    def pack_spec(grp):
        last = spec[grp, :, 4 * LN :]
        parts = [last[8 * b : 8 * b + 8] for b in range(parts_of)]
        for q in range(NX):
            piece[grp, q, 0:ST] = spec[grp, :, q * LN : (q + 1) * LN]
            piece[grp, q, ST : ST + 8] = pick(parts, q)

    def pack_bins(grp, n, blocks):
        parts = [blocks[4][8 * b : 8 * b + 8] for b in range(parts_of)]
        for q in range(NX):
            piece_sum[grp, n, q, 0:ST] = pick(blocks[:4], q)
            piece_sum[grp, n, q, ST : ST + 8] = pick(parts, q)

    def take_spec(grp, pieces):
        for q in range(NX):
            spec[grp, :, q * LN : (q + 1) * LN] = pieces[q][0:ST]
        parts = [pieces[q][ST : ST + 8] for q in range(NX)]
        for b in range(parts_of):
            spec[grp, 8 * b : 8 * b + 8, 4 * LN :] = pick(parts, b)

    def take_bins(pieces):
        full = [p[0:ST] for p in pieces]
        parts = [p[ST : ST + 8] for p in pieces]
        out = [pick(full, j) for j in range(4)]
        out.append(jnp.concatenate([pick(parts, b) for b in range(parts_of)], axis=0))
        return out

    def program(grp):
        def go(name, source, target, device):
            c = copy((grp,) + name, source, target, device)
            c.start()
            return c

        def spectrum_of(i, _):
            at = pl.ds(pl.multiple_of(i * STEP, STEP), STEP)
            spec[grp, at] = to_spectrum(load(direct, grp, i, NT), into, spread)
            return 0

        if grp == 0:
            for c in loads[:3]:
                c.wait()
        lax.fori_loop(0, ST // STEP, spectrum_of, 0, unroll=True)
        if grp == 0:
            pl.semaphore_wait(barrier, len(peers))
            for c in swap[:2]:
                c.start()

        for it in range(ITERS):
            pack_spec(grp)
            sent = []
            stage = {}
            for n in (3, 4, 1, 2, 0):
                for o in (2, 1, 3, 0):
                    if n or o:
                        c = go(
                            ("g", n, o), piece.at[grp, freqs[o]], land_g.at[grp, n, f],
                            at_src(0, near[n], o),
                        )
                        stage.setdefault(n, []).append(c)
                        sent.append(c)
            land_g[grp, 0, f] = piece[grp, f]
            late = []

            def arrive(n):
                for c in stage[n]:
                    c.wait_recv()
                at = rows_at(-near[n])
                blocks = take_bins([land_g[grp, n, q] for q in range(NX)])
                for j in range(BL):
                    xs[grp, j, at] = blocks[j]
                return at

            def forward_to(name, at, dz):
                c = go(name, xs.at[grp, :, at], xs.at[grp, :, at], at_src(0, dz))
                late.append(c)
                sent.append(c)

            if it == 0 and grp == GROUPS - 1:
                prepare_onsets()
                for c in loads[3:]:
                    c.wait()
            yield
            for n, w, way in ((3, 0, 1), (4, 1, -1)):
                at = arrive(n)
                forward_to(("g3", n), at, way)
                forward_to(("g4", n), rows_at(-2 * way, w), 2 * way)
            if it == 0 and grp == 0:
                for c in swap[2:]:
                    c.start()
            for n in (1, 2, 0):
                arrive(n)
            yield
            for c in late:
                c.wait_recv()
            owed = list(sent)

            def forward(j, g_at):
                x_high, x_low = halves(unfold(xs[g_at, j]))
                both = mm(r_high[j], jnp.concatenate([x_high, x_low], axis=1))
                g = fold(both[:, :LN] + both[:, LN:] + mm(r_low[j], x_high))
                n = 2 * SRC // SH
                real = is_real((n, LN))
                turned = swap_parts(g[n:], real)
                y[g_at, j] = g[:n] + jnp.where(real, -turned, turned)
                return 0

            if it == 0:
                yield
            for j in range(BL):
                if it:
                    forward(j, grp)
                elif grp == 0:
                    swap[j].wait_recv()
                    prepare(j)
                    for g_at in range(GROUPS):
                        forward(j, g_at)

            order = (2, 3, 1, 0)
            pair = {
                n: go(
                    ("ra", n), y.at[grp, :, rcv_rows(*column[n], 1)], r4a.at[grp, n],
                    at_rcv(0, 0, 1),
                )
                for n in order
            }
            yield
            stage = []
            for n in order:
                pair[n].wait_recv()
                total = y[grp, :, rcv_rows(*column[n], 0)] + r4a[grp, n]
                pack_bins(grp, n, [total[j] for j in range(BL)])
                for o in (2, 1, 3, 0):
                    if n or o:
                        stage.append(
                            go(
                                ("rx", n, o), piece_sum.at[grp, n, freqs[o]],
                                land_r.at[grp, n, f], at_rcv(*column[n], 0, o),
                            )
                        )
            land_r[grp, 0, f] = piece_sum[grp, 0, f]
            yield
            for c in stage:
                c.wait_recv()
            owed += list(pair.values()) + stage
            take_spec(
                grp,
                [
                    (land_r[grp, 0, q] + land_r[grp, 1, q]) + (land_r[grp, 2, q] + land_r[grp, 3, q])
                    for q in range(NX)
                ],
            )

            def up(i, _):
                at = pl.ds(pl.multiple_of(i * STEP, STEP), STEP)
                x = jnp.where(keep(1, grp, i), to_time(spec[grp, at], collect, back), 0.0)
                store(out_minus, grp, i, x)
                spec[grp, at] = to_spectrum(x, into, spread)
                return 0

            lax.fori_loop(0, ST // STEP, up, 0, unroll=True)

            for c in owed:
                c.wait_send()
            owed = []
            pack_spec(grp)
            stage = {}
            for n in order:
                for o in (2, 1, 3, 0):
                    if n or o:
                        c = go(
                            ("cx", n, o), piece.at[grp, freqs[o]], land_f.at[grp, n, f],
                            at_rcv(*column[n], 0, o),
                        )
                        stage.setdefault(n, []).append(c)
            land_f[grp, 0, f] = piece[grp, f]
            yield
            pair = []
            for n in (0, 1, 3, 2):
                for c in stage[n]:
                    c.wait_recv()
                at = rcv_rows(*column[n], 0)
                blocks = take_bins([land_f[grp, n, q] for q in range(NX)])
                for j in range(BL):
                    cs[grp, j, at] = blocks[j]
                pair.append(
                    go(("cc", n), cs.at[grp, :, at], cs.at[grp, :, at], at_rcv(0, 0, 1))
                )
            yield
            for c in pair:
                c.wait_recv()
            owed += pair + [c for n in order for c in stage[n]]

            def adjoint(j, _):
                block = cs[grp, j]
                real = is_real(block.shape)
                turned = swap_parts(block, real)
                both = jnp.concatenate([block, jnp.where(real, turned, -turned)], axis=0)
                c_high, c_low = halves(unfold(both))
                both = mm(t_high[j], jnp.concatenate([c_high, c_low], axis=1))
                h[grp, j] = fold(both[:, :LN] + both[:, LN:] + mm(t_low[j], c_high))
                return 0

            for j in range(BL):
                adjoint(j, 0)

            sent = []
            owed_now, owed = owed, []
            stage = [[], []]

            def part_to(name, w, slot, dist, dz, part=None):
                target = rs.at[grp, slot]
                if part is not None:
                    target = rs.at[grp, slot, :, pl.ds(part * (ST // 2), ST // 2)]
                c = go(name, h.at[grp, :, rows_at(dist, part)], target, at_src(0, dz))
                stage[w].append(c)
                sent.append(c)

            for w, way in ((0, 1), (1, -1)):
                part_to(("s4", w), w, 2 + w, 4, 2 * way, w)
                part_to(("s3", w), w, w, 3 * way, way)

            last = {}

            def finish(n, blocks):
                pack_bins(grp, n, blocks)
                for o in (2, 1, 3, 0):
                    if n or o:
                        c = go(
                            ("sx", n, o), piece_sum.at[grp, n, freqs[o]], land_s.at[grp, n, f],
                            at_src(0, near[n], o),
                        )
                        last.setdefault(n, []).append(c)
                        sent.append(c)

            def bins_of(total):
                return [total[j] for j in range(BL)]

            for c in owed_now:
                c.wait_send()
            finish(1, [h[grp, j, rows_at(1)] for j in range(BL)])
            finish(2, [h[grp, j, rows_at(-1)] for j in range(BL)])
            finish(0, [h[grp, j, rows_at(0)] for j in range(BL)])
            land_s[grp, 0, f] = piece_sum[grp, 0, f]
            yield
            for w, way in ((0, 1), (1, -1)):
                for c in stage[w]:
                    c.wait_recv()
                total = h[grp, :, rows_at(2 * way)] + rs[grp, w]
                half = slice(w * (ST // 2), (w + 1) * (ST // 2))
                some = [total[:, : ST // 2], total[:, ST // 2 :]]
                some[w] = some[w] + rs[grp, 2 + w, :, half]
                finish(3 + w, bins_of(jnp.concatenate(some, axis=1)))
            yield
            for n in range(5):
                for c in last[n]:
                    c.wait_recv()
            pieces = []
            for q in range(NX):
                total = land_s[grp, 0, q]
                for n in range(1, 5):
                    total = total + land_s[grp, n, q]
                pieces.append(total)
            take_spec(grp, pieces)

            def down(i, _):
                at = pl.ds(pl.multiple_of(i * STEP, STEP), STEP)
                x = jnp.where(keep(0, grp, i), to_time(spec[grp, at], collect, back), 0.0)
                x = load(direct, grp, i, NT) + x
                if it < ITERS - 1:
                    spec[grp, at] = to_spectrum(x, into, spread)
                else:
                    store(out_plus, grp, i, x)
                return 0

            lax.fori_loop(0, ST // STEP, down, 0, unroll=True)
            for c in sent:
                c.wait_send()

    running = [program(grp) for grp in range(GROUPS)]
    while running:
        for p in list(running):
            if next(p, 0) == 0:
                running.remove(p)
    for c in swap:
        c.wait_send()


MESSAGES = 84 * GROUPS + BL


def per_device(direct, reflection, onset_plus, onset_minus):
    vmem = pl.BlockSpec(memory_space=pltpu.VMEM)
    hbm = pl.BlockSpec(memory_space=pl.ANY)
    f32, bf16 = jnp.float32, jnp.bfloat16
    traces = pltpu.VMEM((ST * SH, FP, NT), f32)
    return pl.pallas_call(
        kernel,
        out_shape=(traces, traces),
        in_specs=[hbm, hbm, vmem, vmem, hbm, hbm, hbm, hbm],
        out_specs=(vmem, vmem),
        scratch_shapes=[
            pltpu.VMEM((ST * SH, FP, NT), f32),
            pltpu.VMEM((2, BL, SRC, HALF), f32),
            pltpu.VMEM((2, NT, LN), bf16),
            pltpu.VMEM((LN, WIDE), bf16),
            pltpu.VMEM((2, WIDE, LN), bf16),
            pltpu.VMEM((LN, NT), bf16),
            pltpu.SemaphoreType.DMA((6 + 2 * GROUPS,)),
            pltpu.VMEM((BL, 2, SRC, HALF), f32),
            pltpu.VMEM((BL, 4 * SRC, HALF), bf16),
            pltpu.VMEM((BL, 4 * SRC, HALF), bf16),
            pltpu.VMEM((BL, HALF, 4 * SRC), bf16),
            pltpu.VMEM((BL, HALF, 4 * SRC), bf16),
            pltpu.VMEM((2, ST * SH, FP, LN), f32),
            pltpu.VMEM((GROUPS, ST, WIDE), f32),
            pltpu.VMEM((GROUPS, NX, PR, LN), f32),
            pltpu.VMEM((GROUPS, 5, NX, PR, LN), f32),
            pltpu.VMEM((GROUPS, 5, NX, PR, LN), f32),
            pltpu.VMEM((GROUPS, 4, NX, PR, LN), f32),
            pltpu.VMEM((GROUPS, 4, NX, PR, LN), f32),
            pltpu.VMEM((GROUPS, 5, NX, PR, LN), f32),
            pltpu.VMEM((GROUPS, BL, NZ * ST, LN), f32),
            pltpu.VMEM((GROUPS, BL, NY * ST, LN), f32),
            pltpu.VMEM((GROUPS, 4, BL, ST, LN), f32),
            pltpu.VMEM((GROUPS, BL, NY * ST, LN), f32),
            pltpu.VMEM((GROUPS, BL, NZ * ST, LN), f32),
            pltpu.VMEM((GROUPS, 4, BL, ST, LN), f32),
            pltpu.SemaphoreType.DMA((MESSAGES,)),
            pltpu.SemaphoreType.DMA((MESSAGES,)),
        ],
        compiler_params=pltpu.CompilerParams(
            collective_id=0, has_side_effects=True, vmem_limit_bytes=58 * 1024 * 1024
        ),
    )(direct, reflection, onset_plus.T, onset_minus.T, *[jnp.asarray(a) for a in tables()])


def solution(mesh):
    in_specs = (
        P(("rcv", "src"), "freq", None),
        P(None, "freq", "src", "rcv"),
        P(("rcv", "src"), "freq"),
        P(("src", "rcv"), "freq"),
    )
    out_specs = (P(("rcv", "src"), "freq", None), P(("src", "rcv"), "freq", None))
    return jax.shard_map(
        per_device, mesh=mesh, in_specs=in_specs, out_specs=out_specs, check_vma=False
    )
```
